256 devices in a mesh: lat: 64 (over z, x_lo, y), lon: 4 (over x_hi, core).
Axes of the slice: x: 4 (x_hi: 2, x_lo: 2; x = x_hi * 2 + x_lo), y: 4, z: 8, core: 2. Of those that a mesh axis runs over, the one named last changes fastest.
Arguments:
- tokens: bfloat16 [768, 96, 2, 512], P('lat', 'lon'), may hold values from -6 to 6
- land_sea: int32 [768, 96], P('lat', 'lon'), may hold values from 0 to 2
- surface_embed: float32 [3, 512], replicated, may hold values from -4 to 4
- level_table: int32 [2], replicated, may hold values from 0 to 12
- level_embed: float32 [13, 512], replicated, may hold values from -4 to 4
- gain1: float32 [512], replicated, may hold values from 0.25 to 1.75
- w_qkv1: bfloat16 [512, 1536], P(None, 'lat'), may hold values from -0.25 to 0.25
- bias1: float32 [16, 20736], replicated, may hold values from -4 to 4
- w_out1: bfloat16 [512, 512], P(None, 'lat'), may hold values from -0.25 to 0.25
- gain_merge: float32 [2048], replicated, may hold values from 0.25 to 1.75
- w_merge: bfloat16 [2048, 1024], P(None, 'lat'), may hold values from -0.125 to 0.125
- gain2: float32 [1024], replicated, may hold values from 0.25 to 1.75
- w_qkv2: bfloat16 [1024, 3072], P(None, 'lat'), may hold values from -0.1875 to 0.1875
- bias2: float32 [32, 20736], replicated, may hold values from -4 to 4
- w_out2: bfloat16 [1024, 1024], P(None, 'lat'), may hold values from -0.1875 to 0.1875
Outputs:
- level_one: bfloat16 [768, 96, 2, 512], P('lat', 'lon')
- level_two: bfloat16 [384, 48, 2, 1024], P('lat', 'lon')
The draws below stay inside these ranges and needn't reach their ends.
All inputs are finite; a program needn't handle non-finite values.
Results may differ from the reference program's by a relative error of at most 0.011.
Values may be sent and summed in bfloat16 or wider, within the bound.
A program may use at most 192 MiB of HBM per device.

```python
import jax
import jax.numpy as jnp
from jax import lax

D = 512
LV = 2
PLEVELS = 13
SURFACES = 3
WZ = 2
WL = 6
WN = 12
WT = 144
HEADS1 = 16
HEADS2 = 32
NLAT = 768
NLON = 96


def place_ends(array, stream_key, low, top_value):
    place = [jax.random.randint(jax.random.fold_in(stream_key, axis), (), 0, length) for axis, length in enumerate(array.shape)]
    widest = array.shape.index(max(array.shape))
    neighbour = place[:widest] + [(place[widest] + 1) % array.shape[widest]] + place[widest + 1:]
    return array.at[tuple(place)].set(low).at[tuple(neighbour)].set(top_value)


def level_of(rng, extent, shards, smallest, top_value):
    loudness = 1.0
    for axis_at, blocks in shards:
        heights = jax.random.uniform(jax.random.fold_in(jax.random.fold_in(rng, 6), axis_at), (blocks,), jnp.float32, smallest / len(shards), top_value / len(shards))
        loudness = loudness * jnp.repeat(jnp.exp(heights), extent[axis_at] // blocks).reshape((-1,) + (1,) * (len(extent) - 1 - axis_at))
    return loudness


def bell_draw(rng, dims, deviation, most, split=(), kind=jnp.bfloat16):
    drawn = deviation * jax.random.normal(rng, dims, jnp.float32)
    if split:
        drawn = drawn * level_of(rng, dims, split, -0.22, 0.18)
    return jnp.clip(drawn, -most, most).astype(kind)


def setup_inputs(seed: int = 0) -> dict:
    arg_keys = jax.random.split(jax.random.key(seed), 16)
    tokens = bell_draw(arg_keys[0], (NLAT, NLON, LV, D), 1.0, 6.0, ((0, 64), (1, 4)))
    land_sea = place_ends(jax.random.randint(arg_keys[1], (NLAT, NLON), 0, SURFACES), jax.random.fold_in(arg_keys[1], 1), 0, SURFACES - 1).astype(jnp.int32)
    surface_embed = bell_draw(arg_keys[2], (SURFACES, D), 0.7, 4.0, (), jnp.float32)
    level_table = jax.random.randint(arg_keys[3], (LV,), 0, PLEVELS).astype(jnp.int32)
    level_embed = bell_draw(arg_keys[4], (PLEVELS, D), 0.7, 4.0, (), jnp.float32)
    gain1 = jnp.clip(1.0 + 0.15 * jax.random.normal(arg_keys[5], (D,), jnp.float32), 0.25, 1.75)
    w_qkv1 = bell_draw(arg_keys[6], (D, 3 * D), D ** -0.5, 0.25, ((1, 64),))
    bias1 = bell_draw(arg_keys[7], (HEADS1, WT * WT), 1.0, 4.0, (), jnp.float32)
    w_out1 = bell_draw(arg_keys[8], (D, D), D ** -0.5, 0.25, ((1, 64),))
    gain_merge = jnp.clip(1.0 + 0.15 * jax.random.normal(arg_keys[9], (4 * D,), jnp.float32), 0.25, 1.75)
    w_merge = bell_draw(arg_keys[10], (4 * D, 2 * D), (4 * D) ** -0.5, 0.125, ((1, 64),))
    gain2 = jnp.clip(1.0 + 0.15 * jax.random.normal(arg_keys[11], (2 * D,), jnp.float32), 0.25, 1.75)
    w_qkv2 = bell_draw(arg_keys[12], (2 * D, 6 * D), (2 * D) ** -0.5, 0.1875, ((1, 64),))
    bias2 = bell_draw(arg_keys[13], (HEADS2, WT * WT), 1.0, 4.0, (), jnp.float32)
    w_out2 = bell_draw(arg_keys[14], (2 * D, 2 * D), (2 * D) ** -0.5, 0.1875, ((1, 64),))
    return dict(tokens=tokens, land_sea=land_sea, surface_embed=surface_embed, level_table=level_table, level_embed=level_embed, gain1=gain1, w_qkv1=w_qkv1, bias1=bias1, w_out1=w_out1, gain_merge=gain_merge, w_merge=w_merge, gain2=gain2, w_qkv2=w_qkv2, bias2=bias2, w_out2=w_out2)


def norm_rows(values, gain):
    mean = lax.optimization_barrier(jnp.mean(values, -1, keepdims=True))
    centred = values - mean
    spread = lax.optimization_barrier(jnp.mean(centred * centred, -1, keepdims=True))
    return centred * lax.rsqrt(spread + 1e-05) * gain

def window_attention(qkv, valid, bias, heads):
    rows, cols, levels, triple = qkv.shape
    width = triple // 3
    size = width // heads
    grid = qkv.reshape(rows // WL, WL, cols // WN, WN, levels // WZ, WZ, 3, heads, size)
    grid = grid.transpose(6, 0, 2, 4, 7, 1, 3, 5, 8).reshape(3, -1, heads, WT, size)
    grid = grid.astype(jnp.float32)
    scores = jnp.einsum('whqd,whkd->whqk', grid[0], grid[1]) / jnp.sqrt(jnp.float32(size))
    scores = scores + bias.reshape(heads, WT, WT)[None].astype(jnp.float32)
    keymask = jnp.repeat(valid.reshape(rows // WL, WL), WN * WZ, axis=1)
    keymask = jnp.repeat(keymask, cols // WN * (levels // WZ), axis=0)
    scores = jnp.where(keymask[:, None, None, :], scores, jnp.float32(-1e+30))
    top = lax.optimization_barrier(jnp.max(scores, -1, keepdims=True))
    weights = jnp.exp(scores - top)
    probs = (weights / lax.optimization_barrier(jnp.sum(weights, -1, keepdims=True))).astype(jnp.bfloat16)
    mixed = jnp.einsum('whqk,whkd->whqd', probs.astype(jnp.float32), grid[2]).astype(jnp.bfloat16)
    mixed = mixed.reshape(rows // WL, cols // WN, levels // WZ, heads, WL, WN, WZ, size)
    return mixed.transpose(0, 4, 1, 5, 2, 6, 3, 7).reshape(rows, cols, levels, width)

def shifted_level(normed, w_qkv, bias, heads):
    rows_all, cols_all, levels, width = normed.shape
    half_lat = WL // 2
    half_lon = WN // 2
    rolled = jnp.roll(normed, -half_lon, axis=1)
    padded = jnp.pad(rolled, ((half_lat, half_lat), (0, 0), (0, 0), (0, 0)))
    bands = padded.reshape(-1, WL, cols_all, levels, width)
    count = bands.shape[0]

    def one_band(item):
        band, number = item
        qkv = jnp.dot(band.reshape(-1, width), w_qkv, preferred_element_type=jnp.float32).astype(jnp.bfloat16)
        qkv = qkv.reshape(WL, cols_all, levels, 3 * width)
        position = number * WL + jnp.arange(WL, dtype=jnp.int32)
        valid = (position >= half_lat) & (position < half_lat + rows_all)
        return window_attention(qkv, valid, bias, heads)
    result = lax.map(one_band, (bands, jnp.arange(count, dtype=jnp.int32)))
    result = result.reshape(-1, cols_all, levels, width)[half_lat:half_lat + rows_all]
    return jnp.roll(result, half_lon, axis=1)

def reference(tokens, land_sea, surface_embed, level_table, level_embed, gain1, w_qkv1, bias1, w_out1, gain_merge, w_merge, gain2, w_qkv2, bias2, w_out2):
    rows_all, cols_all, levels, width = tokens.shape
    embedded = tokens.astype(jnp.float32) + surface_embed[land_sea][:, :, None, :] + level_embed[level_table][None, None, :, :]
    normed1 = norm_rows(embedded, gain1).astype(jnp.bfloat16)
    attended1 = shifted_level(normed1, w_qkv1, bias1, HEADS1)
    stream1 = embedded + jnp.dot(attended1.reshape(-1, width), w_out1, preferred_element_type=jnp.float32).reshape(rows_all, cols_all, levels, width)
    level_one = stream1.astype(jnp.bfloat16)
    merged = jnp.concatenate([stream1[0::2, 0::2], stream1[1::2, 0::2], stream1[0::2, 1::2], stream1[1::2, 1::2]], -1)
    mnormed = norm_rows(merged, gain_merge).astype(jnp.bfloat16)
    half_rows = rows_all // 2
    half_cols = cols_all // 2
    stream2 = jnp.dot(mnormed.reshape(-1, 4 * width), w_merge, preferred_element_type=jnp.float32).reshape(half_rows, half_cols, levels, 2 * width)
    normed2 = norm_rows(stream2, gain2).astype(jnp.bfloat16)
    attended2 = shifted_level(normed2, w_qkv2, bias2, HEADS2)
    level_two = stream2 + jnp.dot(attended2.reshape(-1, 2 * width), w_out2, preferred_element_type=jnp.float32).reshape(half_rows, half_cols, levels, 2 * width)
    return (level_one, level_two.astype(jnp.bfloat16))
```

```python
import functools

import jax
import jax.numpy as jnp
from jax import lax
from jax.experimental import pallas as pl
from jax.experimental.pallas import tpu as pltpu
from jax.sharding import PartitionSpec as P

HEAD = 32
WZ = 2
WL = 6
WN = 12
WT = 144
MESH = pl.DeviceIdType.MESH
GROUPS = ((32, 512), (16, 2048), (48, 1024), (16, 1024))
NG = len(GROUPS)
ZS, YS, XS, SS = 0, 7, 11, 19
SLOTS = 32


class Place:
    def __init__(self):
        lat = lax.axis_index("lat")
        lon = lax.axis_index("lon")
        self.lat, self.lon = lat, lon
        self.z = lat // 8
        self.xlo = (lat // 4) % 2
        self.y = lat % 4
        self.xhi = lon // 2
        self.core = lon % 2
        self.x = self.xhi * 2 + self.xlo

    def at(self, x=None, y=None, z=None, core=None):
        x = self.x if x is None else x
        y = self.y if y is None else y
        z = self.z if z is None else z
        core = self.core if core is None else core
        return ((z * 2 + x % 2) * 4 + y, (x // 2) * 2 + core)


class Gather:
    def __init__(self, place, shard, full, send, recv):
        self.p, self.shard, self.full, self.send, self.recv = place, shard, full, send, recv
        p = place
        self.up = p.at(y=(p.y + 1) % 4)
        self.down = p.at(y=(p.y + 3) % 4)
        self.east = p.at(x=(p.x + 1) % 4)
        self.west = p.at(x=(p.x + 3) % 4)
        self.twin = p.at(core=1 - p.core)
        self.partners = [p.at(z=(p.z + d) % 8) for d in range(1, 8)] + [
            self.up, self.down, self.east, self.west, self.twin]

    def copy(self, g, slot, src, dst, to):
        return pltpu.make_async_remote_copy(
            src_ref=src, dst_ref=dst, send_sem=self.send.at[g, slot], recv_sem=self.recv.at[g, slot],
            device_id=to, device_id_type=MESH)

    def move(self, g, slot, to, half, zs, line):
        part = self.full[g].at[half, zs, line]
        self.copy(g, slot, part, part, to).start()

    def landed(self, g, slot, half, zs, line):
        part = self.full[g].at[half, zs, line]
        self.copy(g, slot, part, part, self.twin).wait_recv()

    def line(self, xlo, dy):
        return xlo * 4 + (self.p.y + dy) % 4

    def start(self, g):
        p = self.p
        mine = self.full[g].at[p.core, p.z, self.line(p.xlo, 0)]
        for d in range(1, 8):
            self.copy(g, ZS + d - 1, self.shard[g].at[p.core], mine, p.at(z=(p.z + d) % 8)).start()

    def after_z(self, g):
        p = self.p
        own = self.line(p.xlo, 0)
        mine = self.full[g].at[p.core, p.z, own]
        for d in range(1, 8):
            part = self.full[g].at[p.core, (p.z + 8 - d) % 8, own]
            self.copy(g, ZS + d - 1, part, part, self.twin).wait_recv()
        whole = pl.ds(0, 8)
        self.move(g, YS + 0, self.up, p.core, whole, own)
        self.move(g, YS + 1, self.down, p.core, whole, own)
        self.to_x(g, 0, 0)
        self.to_x(g, 0, 1)
        self.move(g, SS + 0, self.twin, p.core, whole, own)

    def to_x(self, g, dy, part):
        p = self.p
        zs = pl.ds(4 * part, 4)
        self.move(g, XS + 2 * dy + part, (self.east, self.west)[part], p.core, zs, self.line(p.xlo, dy))

    def after_y(self, g):
        p = self.p
        whole = pl.ds(0, 8)
        below, above = self.line(p.xlo, 3), self.line(p.xlo, 1)
        self.landed(g, YS + 0, p.core, whole, below)
        self.move(g, YS + 2, self.up, p.core, pl.ds(0, 4), below)
        self.landed(g, YS + 1, p.core, whole, above)
        self.move(g, YS + 3, self.down, p.core, pl.ds(4, 4), above)
        for dy in (3, 1):
            for part in (0, 1):
                self.to_x(g, dy, part)
        self.move(g, SS + 1, self.twin, p.core, whole, below)
        self.move(g, SS + 2, self.twin, p.core, whole, above)

    def after_far(self, g):
        p = self.p
        far = self.line(p.xlo, 2)
        for part in (0, 1):
            zs = pl.ds(4 * part, 4)
            self.landed(g, YS + 2 + part, p.core, zs, far)
            self.to_x(g, 2, part)
            self.move(g, SS + 3 + part, self.twin, p.core, zs, far)

    def after_x(self, g):
        p = self.p
        for dy in (0, 3, 1, 2):
            for part in (0, 1):
                zs = pl.ds(4 * part, 4)
                line = self.line(1 - p.xlo, dy)
                self.landed(g, XS + 2 * dy + part, p.core, zs, line)
                self.move(g, SS + 5 + 2 * dy + part, self.twin, p.core, zs, line)

    def finish(self, g):
        p = self.p
        half = 1 - p.core
        whole = pl.ds(0, 8)
        self.landed(g, SS + 0, half, whole, self.line(p.xlo, 0))
        self.landed(g, SS + 1, half, whole, self.line(p.xlo, 3))
        self.landed(g, SS + 2, half, whole, self.line(p.xlo, 1))
        for part in (0, 1):
            zs = pl.ds(4 * part, 4)
            self.landed(g, SS + 3 + part, half, zs, self.line(p.xlo, 2))
            for dy in range(4):
                self.landed(g, SS + 5 + 2 * dy + part, half, zs, self.line(1 - p.xlo, dy))

    def drain(self, g):
        p = self.p

        def sent(slot, src):
            self.copy(g, slot, src, src, self.twin).wait_send()

        for d in range(1, 8):
            sent(ZS + d - 1, self.shard[g].at[p.core])
        whole = self.full[g].at[p.core, pl.ds(0, 8), 0]
        half = self.full[g].at[p.core, pl.ds(0, 4), 0]
        for slot in (YS, YS + 1, SS, SS + 1, SS + 2):
            sent(slot, whole)
        for slot in (YS + 2, YS + 3, SS + 3, SS + 4):
            sent(slot, half)
        for k in range(8):
            sent(XS + k, half)
            sent(SS + 5 + k, half)


def gather_kernel(*refs):
    shard, out = refs[:NG], refs[NG:2 * NG]
    full = refs[2 * NG:3 * NG]
    send, recv, local = refs[3 * NG:]
    place = Place()
    net = Gather(place, shard, full, send, recv)
    barrier = pltpu.get_barrier_semaphore()
    for to in net.partners:
        pl.semaphore_signal(barrier, inc=1, device_id=to, device_id_type=MESH)
    pl.semaphore_wait(barrier, len(net.partners))
    for g in range(NG):
        own = pltpu.make_async_copy(
            shard[g].at[place.core], full[g].at[place.core, place.z, net.line(place.xlo, 0)], local.at[g])
        own.start()
        net.start(g)
        own.wait()
    for step in range(NG + 4):
        for k, act in enumerate((net.after_z, net.after_y, net.after_far, net.after_x, net.finish)):
            g = step - k
            if 0 <= g < NG:
                act(g)
    for g in range(NG):
        pltpu.make_async_copy(full[g], out[g], local.at[g]).start()
    for g in range(NG):
        net.drain(g)
    for g in range(NG):
        pltpu.make_async_copy(full[g], out[g], local.at[g]).wait()


def gather_weights(w_qkv1, w_out1, w_merge, w_qkv2, w_out2):
    shards = [jnp.concatenate([w_qkv1, w_out1], 1), w_merge, w_qkv2, w_out2]
    shards = [w.T.reshape(w.shape[1], 2, w.shape[0] // 2).transpose(1, 0, 2) for w in shards]
    shapes = [(2, 8, 8, rows, depth // 2) for rows, depth in GROUPS]
    full = pl.pallas_call(
        gather_kernel,
        out_shape=[jax.ShapeDtypeStruct(s, jnp.bfloat16) for s in shapes],
        in_specs=[pl.BlockSpec(memory_space=pltpu.VMEM)] * NG,
        out_specs=[pl.BlockSpec(memory_space=pl.ANY)] * NG,
        scratch_shapes=[pltpu.VMEM(s, jnp.bfloat16) for s in shapes] + [
            pltpu.SemaphoreType.DMA((NG, SLOTS)),
            pltpu.SemaphoreType.DMA((NG, SLOTS)),
            pltpu.SemaphoreType.DMA((NG,)),
        ],
        compiler_params=pltpu.CompilerParams(
            collective_id=0, has_side_effects=True, vmem_limit_bytes=40 * 2**20),
    )(*shards)
    whole = [f.reshape(2, 64, rows, depth // 2) for f, (rows, depth) in zip(full, GROUPS)]

    def columns(f, first, last):
        return f[:, :, first:last].transpose(0, 3, 1, 2).reshape(-1, 64 * (last - first))

    return (
        columns(whole[0], 0, 24),
        columns(whole[0], 24, 32),
        columns(whole[1], 0, 16),
        columns(whole[2], 0, 48),
        columns(whole[3], 0, 16),
    )


def passed_along(block, axis, distance):
    devices = range(lax.axis_size(axis))
    route = [((i - distance) % len(devices), i) for i in devices]
    return lax.ppermute(block, axis, route)


def from_behind(value, axis, steps):
    count = lax.axis_size(axis)
    initial, last = (max(0, -steps), min(count, count - steps))
    return lax.ppermute(value, axis, [(source, source + steps) for source in range(initial, last)])


def norm_rows(values, gain):
    mean = jnp.mean(values, -1, keepdims=True)
    centred = values - mean
    spread = jnp.mean(centred * centred, -1, keepdims=True)
    return centred * lax.rsqrt(spread + 1e-05) * gain


def window_attention(qkv, valid, bias, heads):
    rows, cols, levels, triple = qkv.shape
    width = triple // 3
    size = width // heads
    grid = qkv.reshape(rows // WL, WL, cols // WN, WN, levels // WZ, WZ, 3, heads, size)
    grid = grid.transpose(6, 0, 2, 4, 7, 1, 3, 5, 8).reshape(3, -1, heads, WT, size)
    scores = jnp.einsum(
        "whqd,whkd->whqk", grid[0], grid[1], preferred_element_type=jnp.float32
    ) / jnp.sqrt(jnp.float32(size))
    scores = scores + bias.reshape(heads, WT, WT)[None]
    keymask = jnp.repeat(valid.reshape(rows // WL, WL), WN * WZ, axis=1)
    keymask = jnp.repeat(keymask, cols // WN * (levels // WZ), axis=0)
    scores = jnp.where(keymask[:, None, None, :], scores, jnp.float32(-1e30))
    top = jnp.max(scores, -1, keepdims=True)
    weights = jnp.exp(scores - top)
    probs = (weights / jnp.sum(weights, -1, keepdims=True)).astype(jnp.bfloat16)
    mixed = jnp.einsum(
        "whqk,whkd->whqd", probs, grid[2], preferred_element_type=jnp.float32
    ).astype(jnp.bfloat16)
    mixed = mixed.reshape(rows // WL, cols // WN, levels // WZ, heads, WL, WN, WZ, size)
    return mixed.transpose(0, 4, 1, 5, 2, 6, 3, 7).reshape(rows, cols, levels, width)


def shifted_level(normed, w_qkv, bias, heads):
    lat_dev, lon_dev, levels, width = normed.shape
    half_lat = WL // 2
    half_lon = WN // 2
    lat_index = lax.axis_index("lat")
    lat_count = lax.axis_size("lat")
    beyond = passed_along(normed[:, :half_lon], "lon", -1)
    widened = jnp.concatenate([normed[:, half_lon:], beyond], 1)
    below = from_behind(widened[:half_lat], "lat", -1)
    padding = jnp.zeros((half_lat,) + widened.shape[1:], normed.dtype)
    padded = jnp.concatenate([padding, widened, below], 0)
    rows = padded.shape[0]
    qkv = jnp.dot(padded.reshape(-1, width), w_qkv, preferred_element_type=jnp.float32)
    qkv = qkv.astype(jnp.bfloat16).reshape(rows, lon_dev, levels, 3 * width)
    position = jnp.arange(rows, dtype=jnp.int32)
    valid = (position >= half_lat) & ((position < half_lat + lat_dev) | (lat_index < lat_count - 1))
    attended = window_attention(qkv, valid, bias, heads)
    returned = from_behind(attended[half_lat + lat_dev :], "lat", 1)
    leading = jnp.where(lat_index == 0, attended[half_lat : 2 * half_lat], returned)
    stacked = jnp.concatenate([leading, attended[2 * half_lat : half_lat + lat_dev]], 0)
    wrapped = passed_along(stacked[:, lon_dev - half_lon :], "lon", 1)
    return jnp.concatenate([wrapped, stacked[:, : lon_dev - half_lon]], 1)


def shards(
    tokens, land_sea, surface_embed, level_table, level_embed, gain1, w_qkv1, bias1, w_out1,
    gain_merge, w_merge, gain2, w_qkv2, bias2, w_out2,
):
    lat_dev, lon_dev, levels, width = tokens.shape
    w_qkv1, w_out1, w_merge, w_qkv2, w_out2 = gather_weights(w_qkv1, w_out1, w_merge, w_qkv2, w_out2)

    def product(flat, weight):
        return jnp.dot(flat, weight, preferred_element_type=jnp.float32)

    kinds = surface_embed.shape[0]
    surface_hot = (land_sea[..., None] == jnp.arange(kinds, dtype=jnp.int32)).astype(jnp.float32)
    surface = jnp.dot(
        surface_hot.reshape(-1, kinds), surface_embed, precision=lax.Precision.HIGHEST
    ).reshape(lat_dev, lon_dev, 1, width)
    level_hot = (level_table[:, None] == jnp.arange(level_embed.shape[0], dtype=jnp.int32)).astype(
        jnp.float32
    )
    level_rows = jnp.dot(level_hot, level_embed, precision=lax.Precision.HIGHEST)
    embedded = tokens.astype(jnp.float32) + surface + level_rows[None, None]
    normed1 = norm_rows(embedded, gain1).astype(jnp.bfloat16)
    attended1 = shifted_level(normed1, w_qkv1, bias1, width // HEAD)
    stream1 = embedded + product(attended1.reshape(-1, width), w_out1).reshape(
        lat_dev, lon_dev, levels, width
    )
    level_one = stream1.astype(jnp.bfloat16)
    merged = jnp.concatenate(
        [stream1[0::2, 0::2], stream1[1::2, 0::2], stream1[0::2, 1::2], stream1[1::2, 1::2]], -1
    )
    mnormed = norm_rows(merged, gain_merge).astype(jnp.bfloat16)
    half_rows = lat_dev // 2
    half_cols = lon_dev // 2
    stream2 = product(mnormed.reshape(-1, 4 * width), w_merge).reshape(
        half_rows, half_cols, levels, 2 * width
    )
    normed2 = norm_rows(stream2, gain2).astype(jnp.bfloat16)
    attended2 = shifted_level(normed2, w_qkv2, bias2, 2 * width // HEAD)
    level_two = stream2 + product(attended2.reshape(-1, 2 * width), w_out2).reshape(
        half_rows, half_cols, levels, 2 * width
    )
    return (level_one, level_two.astype(jnp.bfloat16))


def solution(mesh):
    placed = (
        P("lat", "lon", None, None), P("lat", "lon"), P(), P(), P(), P(),
        P(None, "lat"), P(), P(None, "lat"), P(), P(None, "lat"), P(), P(None, "lat"), P(), P(None, "lat"),
    )
    return jax.shard_map(
        shards,
        mesh=mesh,
        in_specs=placed,
        out_specs=(P("lat", "lon", None, None), P("lat", "lon", None, None)),
        check_vma=False,
    )
```

```python
import jax
import jax.numpy as jnp
from jax import lax
from jax.experimental import pallas as pl
from jax.experimental.pallas import tpu as pltpu
from jax.sharding import PartitionSpec as P

WT = 144
NT = (((1,), (1,)), ((), ()))
LOG2E = 1.4426950408889634
ABSENT = -1e30
MESH = pl.DeviceIdType.MESH
GROUPS = ((32, 512), (16, 2048), (48, 1024), (16, 1024))
NG = len(GROUPS)
ZS, YS, XS, SS = 0, 7, 11, 19
SLOTS = 32


class Place:
    def __init__(self):
        lat = lax.axis_index("lat")
        lon = lax.axis_index("lon")
        self.lat, self.lon = lat, lon
        self.z = lat // 8
        self.xlo = (lat // 4) % 2
        self.y = lat % 4
        self.xhi = lon // 2
        self.core = lon % 2
        self.x = self.xhi * 2 + self.xlo

    def at(self, x=None, y=None, z=None, core=None):
        x = self.x if x is None else x
        y = self.y if y is None else y
        z = self.z if z is None else z
        core = self.core if core is None else core
        return ((z * 2 + x % 2) * 4 + y, (x // 2) * 2 + core)


class Gather:
    def __init__(self, place, shard, full, send, recv):
        self.p, self.shard, self.full, self.send, self.recv = place, shard, full, send, recv
        p = place
        self.up = p.at(y=(p.y + 1) % 4)
        self.down = p.at(y=(p.y + 3) % 4)
        self.east = p.at(x=(p.x + 1) % 4)
        self.west = p.at(x=(p.x + 3) % 4)
        self.twin = p.at(core=1 - p.core)
        self.partners = [p.at(z=(p.z + d) % 8) for d in range(1, 8)] + [
            self.up, self.down, self.east, self.west, self.twin]

    def copy(self, g, slot, src, dst, to):
        return pltpu.make_async_remote_copy(
            src_ref=src, dst_ref=dst, send_sem=self.send.at[g, slot], recv_sem=self.recv.at[g, slot],
            device_id=to, device_id_type=MESH)

    def move(self, g, slot, to, half, zs, line):
        part = self.full[g].at[half, zs, line]
        self.copy(g, slot, part, part, to).start()

    def landed(self, g, slot, half, zs, line):
        part = self.full[g].at[half, zs, line]
        self.copy(g, slot, part, part, self.twin).wait_recv()

    def line(self, xlo, dy):
        return xlo * 4 + (self.p.y + dy) % 4

    def start(self, g):
        p = self.p
        mine = self.full[g].at[p.core, p.z, self.line(p.xlo, 0)]
        for d in range(1, 8):
            self.copy(g, ZS + d - 1, self.shard[g].at[p.core], mine, p.at(z=(p.z + d) % 8)).start()

    def after_z(self, g):
        p = self.p
        own = self.line(p.xlo, 0)
        mine = self.full[g].at[p.core, p.z, own]
        for d in range(1, 8):
            part = self.full[g].at[p.core, (p.z + 8 - d) % 8, own]
            self.copy(g, ZS + d - 1, part, part, self.twin).wait_recv()
        whole = pl.ds(0, 8)
        self.move(g, YS + 0, self.up, p.core, whole, own)
        self.move(g, YS + 1, self.down, p.core, whole, own)
        self.to_x(g, 0, 0)
        self.to_x(g, 0, 1)
        self.move(g, SS + 0, self.twin, p.core, whole, own)

    def to_x(self, g, dy, part):
        p = self.p
        zs = pl.ds(4 * part, 4)
        self.move(g, XS + 2 * dy + part, (self.east, self.west)[part], p.core, zs, self.line(p.xlo, dy))

    def after_y(self, g):
        p = self.p
        whole = pl.ds(0, 8)
        below, above = self.line(p.xlo, 3), self.line(p.xlo, 1)
        self.landed(g, YS + 0, p.core, whole, below)
        self.move(g, YS + 2, self.up, p.core, pl.ds(0, 4), below)
        self.landed(g, YS + 1, p.core, whole, above)
        self.move(g, YS + 3, self.down, p.core, pl.ds(4, 4), above)
        for dy in (3, 1):
            for part in (0, 1):
                self.to_x(g, dy, part)
        self.move(g, SS + 1, self.twin, p.core, whole, below)
        self.move(g, SS + 2, self.twin, p.core, whole, above)

    def after_far(self, g):
        p = self.p
        far = self.line(p.xlo, 2)
        for part in (0, 1):
            zs = pl.ds(4 * part, 4)
            self.landed(g, YS + 2 + part, p.core, zs, far)
            self.to_x(g, 2, part)
            self.move(g, SS + 3 + part, self.twin, p.core, zs, far)

    def after_x(self, g):
        p = self.p
        for dy in (0, 3, 1, 2):
            for part in (0, 1):
                zs = pl.ds(4 * part, 4)
                line = self.line(1 - p.xlo, dy)
                self.landed(g, XS + 2 * dy + part, p.core, zs, line)
                self.move(g, SS + 5 + 2 * dy + part, self.twin, p.core, zs, line)

    def finish(self, g):
        p = self.p
        half = 1 - p.core
        whole = pl.ds(0, 8)
        self.landed(g, SS + 0, half, whole, self.line(p.xlo, 0))
        self.landed(g, SS + 1, half, whole, self.line(p.xlo, 3))
        self.landed(g, SS + 2, half, whole, self.line(p.xlo, 1))
        for part in (0, 1):
            zs = pl.ds(4 * part, 4)
            self.landed(g, SS + 3 + part, half, zs, self.line(p.xlo, 2))
            for dy in range(4):
                self.landed(g, SS + 5 + 2 * dy + part, half, zs, self.line(1 - p.xlo, dy))

    def drain(self, g):
        p = self.p

        def sent(slot, src):
            self.copy(g, slot, src, src, self.twin).wait_send()

        for d in range(1, 8):
            sent(ZS + d - 1, self.shard[g].at[p.core])
        whole = self.full[g].at[p.core, pl.ds(0, 8), 0]
        half = self.full[g].at[p.core, pl.ds(0, 4), 0]
        for slot in (YS, YS + 1, SS, SS + 1, SS + 2):
            sent(slot, whole)
        for slot in (YS + 2, YS + 3, SS + 3, SS + 4):
            sent(slot, half)
        for k in range(8):
            sent(XS + k, half)
            sent(SS + 5 + k, half)


def times(a, b):
    return lax.dot_general(a, b, NT, preferred_element_type=jnp.float32)


def norm_groups(parts, gain):
    width = 128 * len(parts)
    mean = jnp.sum(sum(parts), -1, keepdims=True) / width
    parts = [p - mean for p in parts]
    spread = jnp.sum(sum(p * p for p in parts), -1, keepdims=True) / width
    scale = lax.rsqrt(spread + 1e-05)
    return [p * scale * gain[:, 128 * k:128 * k + 128] for k, p in enumerate(parts)]


def prepare_bias(flat, table, heads):
    lane = lax.broadcasted_iota(jnp.int32, (8, 128), 1)

    def eight(i, _):
        t, q = i // 18, i % 18
        rows = pl.ds(pl.multiple_of(t * 8, 8), 8)
        block = flat[rows, pl.ds(pl.multiple_of(q * 1152, 128), 1152)] * LOG2E
        for s in range(8):
            first, second = block[:, 128 * s:128 * s + 128], block[:, 128 * s + 128:128 * s + 256]
            if s:
                first, second = pltpu.roll(first, 128 - 16 * s, 1), pltpu.roll(second, 128 - 16 * s, 1)
                first = jnp.where(lane < 128 - 16 * s, first, second)
            second = jnp.where(lane < 16, second, ABSENT)
            where = pl.ds(t * 8 * WT + q * 8 + s, 8, stride=WT)
            table[0, where, :] = first
            table[1, where, :] = second
        return 0

    lax.fori_loop(0, heads // 8 * 18, eight, 0)


def attend(q, k, v, bias0, bias1, mask):
    lane = lax.broadcasted_iota(jnp.int32, (WT, 128), 1) // 32
    none = jnp.zeros((256 - WT, 128), jnp.bfloat16)
    heads = jnp.concatenate([jnp.where(lane == h, q, jnp.zeros_like(q)) for h in range(4)], 0)
    scores = times(heads, jnp.concatenate([k, none], 0)) * (LOG2E / 32 ** 0.5)
    bias = jnp.concatenate([bias0, bias1], 1)
    scores = scores + bias + jnp.concatenate([mask] * 4, 0)
    top = jnp.max(scores, -1, keepdims=True)
    weights = jnp.exp2(scores - top).astype(jnp.bfloat16)
    values = jnp.concatenate([jnp.concatenate([v, none], 0), jnp.ones((256, 128), jnp.bfloat16)], 1)
    mixed = jnp.dot(weights, values, preferred_element_type=jnp.float32)
    total, over = mixed[:WT, :128], mixed[:WT, 128:]
    for h in range(1, 4):
        total = jnp.where(lane == h, mixed[WT * h:WT * h + WT, :128], total)
        over = jnp.where(lane == h, mixed[WT * h:WT * h + WT, 128:], over)
    return total / over


def loop(count, step, first=0):
    lax.fori_loop(first, count, lambda i, c: (step(i), c)[1], 0)


def block_kernel(
    shard0, shard1, shard2, shard3, emb, gain1, gain_merge, gain2, bias1_hbm, bias2_hbm,
    one, two,
    full0, full1, full2, full3, flat1, flat2, table1, table2, mask,
    e1, first1, south1, rw1, rn1, rc1, bw1, bn1, bc1, qw, ow, x1, qkv1, s1, mg, mn,
    s2, e2, first2, south2, rw2, rn2, rc2, bw2, bn2, bc2, x2, qkv2,
    sw1, sn1, sc1, sw2, sn2, sc2,
    send, recv, hsend, hrecv, local,
):
    p = Place()
    full = (full0, full1, full2, full3)
    net = Gather(p, (shard0, shard1, shard2, shard3), full, send, recv)
    north, south = (p.lat + 63) % 64, (p.lat + 1) % 64
    west, east = (p.lon + 3) % 4, (p.lon + 1) % 4
    around = [(p.lat, west), (north, p.lon), (north, west), (p.lat, east), (south, p.lon), (south, east)]
    partners = net.partners + around
    barrier = pltpu.get_barrier_semaphore()
    for to in partners:
        pl.semaphore_signal(barrier, inc=1, device_id=to, device_id_type=MESH)
    b1 = pltpu.make_async_copy(bias1_hbm, flat1, local.at[0])
    b2 = pltpu.make_async_copy(bias2_hbm, flat2, local.at[1])
    b1.start()
    b2.start()
    pl.semaphore_wait(barrier, len(partners))

    def neighbour(slot, src, dst, way):
        return pltpu.make_async_remote_copy(
            src_ref=src, dst_ref=dst, send_sem=hsend.at[slot], recv_sem=hrecv.at[slot],
            device_id=around[way], device_id_type=MESH)

    owns = []
    for g in range(NG):
        own = pltpu.make_async_copy(
            net.shard[g].at[p.core], full[g].at[p.core, p.z, net.line(p.xlo, 0)], local.at[2 + g])
        own.start()
        owns.append(own)
    net.start(0)

    sixteen = lax.broadcasted_iota(jnp.int32, (16, 512), 0)
    sixteen2 = lax.broadcasted_iota(jnp.int32, (16, 1024), 0)

    def row_norm(r):
        v = emb[pl.ds(pl.multiple_of(r * 48, 16), 48), :]
        n = norm_groups([v[:, 128 * k:128 * k + 128] for k in range(4)], gain1[...])
        e1[r, 0:8, :] = jnp.zeros((8, 512), jnp.float32)
        e1[r, 48:64, :] = jnp.zeros((16, 512), jnp.float32)
        for k in range(4):
            e1[r, 4:52, 128 * k:128 * k + 128] = n[k]
        first1[r] = e1[r, 0:16, :].astype(jnp.bfloat16)

    loop(12, row_norm)
    for r in range(3):
        south1[r] = e1[r, 16:64, :].astype(jnp.bfloat16)
    halo1 = [neighbour(0, first1.at[pl.ds(3, 9)], rw1, 0), neighbour(1, south1, rn1, 1),
             neighbour(2, first1.at[pl.ds(0, 3)], rc1, 2)]
    for c in halo1:
        c.start()
    for own in owns:
        own.wait()
    net.after_z(0)
    net.start(1)

    half = lambda axis: lax.broadcasted_iota(jnp.int32, (WT, 256), axis) >= WT // 2
    cut = (half(0) != half(1)) & (p.lat == 63)
    mask[0] = jnp.zeros((WT, 256), jnp.float32)
    mask[1] = jnp.where(cut, ABSENT, 0.0)
    b1.wait()
    prepare_bias(flat1, table1, 16)
    net.after_y(0)
    net.after_z(1)
    net.start(2)
    net.after_far(0)
    net.after_y(1)
    b2.wait()
    prepare_bias(flat2, table2, 32)
    net.after_x(0)
    net.after_z(2)
    net.start(3)
    net.after_far(1)

    for c in halo1:
        c.wait_recv()

    def take_west(r):
        e1[r + 3, 48:64, :] = jnp.where(sixteen >= 4, rw1[r].astype(jnp.float32), e1[r + 3, 48:64, :])

    loop(9, take_west)
    for r in range(3):
        n = rn1[r].astype(jnp.float32)
        e1[12 + r, 16:48, :] = n[:32]
        e1[12 + r, 48:64, :] = jnp.where(sixteen >= 4, rc1[r].astype(jnp.float32), n[32:])
    for w in range(4):
        a, b = w // 2, w % 2
        x1[WT * w:WT * w + WT, :] = e1[3 + 6 * a:9 + 6 * a, 16 + 24 * b:40 + 24 * b, :].reshape(
            WT, 512).astype(jnp.bfloat16)

    net.finish(0)

    def unpack(i):
        z, l = i // 4, 2 * (i % 4)
        both = [jnp.concatenate([full0[0, z, l + d], full0[1, z, l + d]], 1).astype(jnp.float32)
                for d in range(2)]
        qw[pl.ds(pl.multiple_of(48 * i, 16), 48), :] = jnp.concatenate(
            [both[0][:24], both[1][:24]], 0).astype(jnp.bfloat16)
        ow[pl.ds(pl.multiple_of(16 * i, 16), 16), :] = jnp.concatenate(
            [both[0][24:], both[1][24:]], 0).astype(jnp.bfloat16)

    loop(32, unpack)

    def project1(n):
        out = times(x1[...], qw[pl.ds(pl.multiple_of(256 * n, 256), 256), :]).astype(jnp.bfloat16)
        qkv1[2 * n] = out[:, :128]
        qkv1[2 * n + 1] = out[:, 128:]

    loop(6, project1)
    net.after_x(1)
    net.after_y(2)
    net.after_z(3)

    def attend1(i):
        w, g = 3 - i // 4, i % 4
        rows = pl.ds(pl.multiple_of(WT * w, 16), WT)
        heads = pl.ds(pl.multiple_of(4 * WT * g, 16), 4 * WT)
        out = attend(qkv1[g, rows, :], qkv1[4 + g, rows, :], qkv1[8 + g, rows, :],
                     table1[0, heads, :], table1[1, heads, :], mask[w // 2])
        e1[pl.ds(3 + 6 * (w // 2), 6), pl.ds(pl.multiple_of(16 + 24 * (w % 2), 8), 24),
           pl.ds(pl.multiple_of(128 * g, 128), 128)] = out.reshape(6, 24, 128)

    loop(8, attend1)
    for r in range(3):
        bn1[r] = e1[12 + r, 16:64, :].astype(jnp.bfloat16)
        bc1[r] = e1[12 + r, 48:64, :].astype(jnp.bfloat16)
    back1 = [neighbour(3, bn1, sn1, 4), neighbour(4, bc1, sc1, 5)]
    for c in back1:
        c.start()
    net.after_far(2)
    net.after_y(3)
    loop(12, attend1, 8)

    def last_columns(r):
        bw1[r] = e1[r + 3, 48:64, :].astype(jnp.bfloat16)

    loop(9, last_columns)
    back1.append(neighbour(5, bw1, sw1, 3))
    back1[2].start()
    net.after_x(2)
    loop(16, attend1, 12)
    net.after_far(3)
    net.finish(1)
    for c in back1:
        c.wait_recv()

    def keep_west(r):
        e1[r + 3, 0:16, :] = jnp.where(sixteen >= 4, sw1[r].astype(jnp.float32), e1[r + 3, 0:16, :])

    loop(9, keep_west)
    for r in range(3):
        e1[r, 16:64, :] = sn1[r].astype(jnp.float32)
        e1[r, 0:16, :] = sc1[r].astype(jnp.float32)

    def collect1(r):
        x1[pl.ds(pl.multiple_of(48 * r, 16), 48), :] = e1[r, 4:52, :].astype(jnp.bfloat16)

    loop(12, collect1)
    for n in range(2):
        cols = slice(256 * n, 256 * n + 256)
        out = emb[:, cols] + times(x1[...], ow[cols, :])
        one[:, cols] = out.astype(jnp.bfloat16)
        s1[2 * n] = out[:, :128]
        s1[2 * n + 1] = out[:, 128:]

    def merge_rows(i):
        for dr in range(2):
            for dc in range(2):
                for level in range(2):
                    for k in range(4):
                        mg[(dc * 2 + dr) * 4 + k, pl.ds(24 * i + level, 12, stride=2), :] = s1[
                            k, pl.ds((2 * i + dr) * 48 + 2 * dc + level, 12, stride=4), :]

    loop(6, merge_rows)

    def merge_norm(c):
        rows = pl.ds(pl.multiple_of(16 * c, 16), 16)
        n = norm_groups([mg[k, rows, :] for k in range(16)], gain_merge[...])
        for k in range(16):
            mn[rows, 128 * k:128 * k + 128] = n[k].astype(jnp.bfloat16)

    loop(9, merge_norm)

    def merge_product(n):
        zs = pl.ds(2 * n, 2)
        out = times(mn[:, :1024], full1[0, zs].reshape(256, 1024))
        out = out + times(mn[:, 1024:], full1[1, zs].reshape(256, 1024))
        s2[2 * n] = out[:, :128]
        s2[2 * n + 1] = out[:, 128:]

    loop(4, merge_product)
    net.after_x(3)

    def row_norm2(r):
        rows = pl.ds(pl.multiple_of(24 * r, 8), 24)
        n = norm_groups([s2[k, rows, :] for k in range(8)], gain2[...])
        e2[r, 0:8, :] = jnp.zeros((8, 1024), jnp.float32)
        e2[r, 24:40, :] = jnp.zeros((16, 1024), jnp.float32)
        for k in range(8):
            e2[r, 4:28, 128 * k:128 * k + 128] = n[k]
        first2[r] = e2[r, 0:16, :].astype(jnp.bfloat16)
        south2[r] = e2[r, 16:32, :].astype(jnp.bfloat16)

    loop(6, row_norm2)
    halo2 = [neighbour(6, first2.at[pl.ds(3, 3)], rw2, 0), neighbour(7, south2.at[pl.ds(0, 3)], rn2, 1),
             neighbour(8, first2.at[pl.ds(0, 3)], rc2, 2)]
    for c in halo2:
        c.start()
    net.finish(2)
    for c in halo2:
        c.wait_recv()
    for r in range(3):
        e2[3 + r, 24:40, :] = jnp.where(sixteen2 >= 4, rw2[r].astype(jnp.float32), e2[3 + r, 24:40, :])
        e2[6 + r, 16:32, :] = rn2[r].astype(jnp.float32)
        e2[6 + r, 24:40, :] = jnp.where(sixteen2 >= 4, rc2[r].astype(jnp.float32), e2[6 + r, 24:40, :])
    x2[...] = e2[3:9, 16:40, :].reshape(WT, 1024).astype(jnp.bfloat16)

    def project2(z):
        out = times(x2[:, :512], full2[0, z].reshape(384, 512))
        out = (out + times(x2[:, 512:], full2[1, z].reshape(384, 512))).astype(jnp.bfloat16)
        for k in range(3):
            qkv2[3 * z + k] = out[:, 128 * k:128 * k + 128]

    loop(8, project2)

    def attend2(g):
        heads = pl.ds(pl.multiple_of(4 * WT * g, 16), 4 * WT)
        out = attend(qkv2[g], qkv2[8 + g], qkv2[16 + g], table2[0, heads, :], table2[1, heads, :], mask[1])
        e2[3:9, 16:40, pl.ds(pl.multiple_of(128 * g, 128), 128)] = out.reshape(6, 24, 128)

    loop(8, attend2)
    for r in range(3):
        bw2[r] = e2[3 + r, 24:40, :].astype(jnp.bfloat16)
        bn2[r] = e2[6 + r, 16:32, :].astype(jnp.bfloat16)
        bc2[r] = e2[6 + r, 24:40, :].astype(jnp.bfloat16)
    back2 = [neighbour(9, bw2, sw2, 3), neighbour(10, bn2, sn2, 4), neighbour(11, bc2, sc2, 5)]
    for c in back2:
        c.start()
    net.finish(3)
    for c in back2:
        c.wait_recv()
    for r in range(3):
        e2[3 + r, 0:16, :] = jnp.where(sixteen2 >= 4, sw2[r].astype(jnp.float32), e2[3 + r, 0:16, :])
        e2[r, 16:32, :] = sn2[r].astype(jnp.float32)
        e2[r, 0:16, :] = sc2[r].astype(jnp.float32)
    for r in range(6):
        x2[24 * r:24 * r + 24, :] = e2[r, 4:28, :].astype(jnp.bfloat16)

    def last(n):
        zs = pl.ds(2 * n, 2)
        out = times(x2[:, :512], full3[0, zs].reshape(256, 512))
        out = out + times(x2[:, 512:], full3[1, zs].reshape(256, 512))
        out = out + jnp.concatenate([s2[2 * n], s2[2 * n + 1]], 1)
        two[:, pl.ds(pl.multiple_of(256 * n, 256), 256)] = out.astype(jnp.bfloat16)

    loop(4, last)
    for c in halo1 + back1 + halo2 + back2:
        c.wait_send()
    for g in range(NG):
        net.drain(g)


def shards(
    tokens, land_sea, surface_embed, level_table, level_embed, gain1, w_qkv1, bias1, w_out1,
    gain_merge, w_merge, gain2, w_qkv2, bias2, w_out2,
):
    weights = [jnp.concatenate([w_qkv1, w_out1], 1), w_merge, w_qkv2, w_out2]
    weights = [w.T.reshape(w.shape[1], 2, w.shape[0] // 2).transpose(1, 0, 2) for w in weights]
    kind = land_sea[:, :, None, None]
    surface = jnp.where(kind == 0, surface_embed[0], jnp.where(kind == 1, surface_embed[1], surface_embed[2]))
    numbers = jnp.arange(level_embed.shape[0], dtype=jnp.int32)
    level_rows = jnp.sum(
        jnp.where((level_table[:, None] == numbers)[:, :, None], level_embed[None], 0.0), 1)
    embedded = tokens.astype(jnp.float32) + surface + level_rows[None, None]
    f32, bf16 = jnp.float32, jnp.bfloat16
    shapes = [(2, 8, 8, rows, depth // 2) for rows, depth in GROUPS]
    scratch = [pltpu.VMEM(s, bf16) for s in shapes] + [pltpu.VMEM(s, t) for s, t in (
        ((16, WT * WT), f32), ((32, WT * WT), f32),
        ((2, 16 * WT, 128), f32), ((2, 32 * WT, 128), f32), ((2, WT, 256), f32),
        ((15, 64, 512), f32), ((12, 16, 512), bf16), ((3, 48, 512), bf16),
        ((9, 16, 512), bf16), ((3, 48, 512), bf16), ((3, 16, 512), bf16),
        ((9, 16, 512), bf16), ((3, 48, 512), bf16), ((3, 16, 512), bf16),
        ((1536, 512), bf16), ((512, 512), bf16), ((576, 512), bf16), ((12, 576, 128), bf16),
        ((4, 576, 128), f32), ((16, WT, 128), f32), ((WT, 2048), bf16),
        ((8, WT, 128), f32), ((9, 40, 1024), f32), ((6, 16, 1024), bf16), ((6, 16, 1024), bf16),
        ((3, 16, 1024), bf16), ((3, 16, 1024), bf16), ((3, 16, 1024), bf16),
        ((3, 16, 1024), bf16), ((3, 16, 1024), bf16), ((3, 16, 1024), bf16),
        ((WT, 1024), bf16), ((24, WT, 128), bf16),
        ((9, 16, 512), bf16), ((3, 48, 512), bf16), ((3, 16, 512), bf16),
        ((3, 16, 1024), bf16), ((3, 16, 1024), bf16), ((3, 16, 1024), bf16),
    )] + [
        pltpu.SemaphoreType.DMA((NG, SLOTS)), pltpu.SemaphoreType.DMA((NG, SLOTS)),
        pltpu.SemaphoreType.DMA((12,)), pltpu.SemaphoreType.DMA((12,)), pltpu.SemaphoreType.DMA((6,)),
    ]
    vmem, anywhere = pl.BlockSpec(memory_space=pltpu.VMEM), pl.BlockSpec(memory_space=pl.ANY)
    one, two = pl.pallas_call(
        block_kernel,
        out_shape=[jax.ShapeDtypeStruct((576, 512), bf16), jax.ShapeDtypeStruct((WT, 1024), bf16)],
        in_specs=[vmem] * 8 + [anywhere] * 2,
        out_specs=[vmem] * 2,
        scratch_shapes=scratch,
        compiler_params=pltpu.CompilerParams(
            collective_id=0, has_side_effects=True, vmem_limit_bytes=60 * 2**20),
    )(*weights, embedded.reshape(576, 512), gain1[None], gain_merge[None], gain2[None], bias1, bias2)
    return one.reshape(12, 24, 2, 512), two.reshape(6, 12, 2, 1024)


def solution(mesh):
    placed = (
        P("lat", "lon", None, None), P("lat", "lon"), P(), P(), P(), P(),
        P(None, "lat"), P(), P(None, "lat"), P(), P(None, "lat"), P(), P(None, "lat"), P(), P(None, "lat"),
    )
    return jax.shard_map(
        shards,
        mesh=mesh,
        in_specs=placed,
        out_specs=(P("lat", "lon", None, None), P("lat", "lon", None, None)),
        check_vma=False,
    )
```

```python
import jax
import jax.numpy as jnp
from jax import lax
from jax.experimental import pallas as pl
from jax.experimental.pallas import tpu as pltpu
from jax.sharding import PartitionSpec as P

WT = 144
NT = (((1,), (1,)), ((), ()))
LOG2E = 1.4426950408889634
ABSENT = -1e30
MESH = pl.DeviceIdType.MESH
GROUPS = ((32, 512), (16, 2048), (48, 1024), (16, 1024))
NG = len(GROUPS)
ZS, YS, XS, SS = 0, 7, 15, 23
SLOTS = 36


class Place:
    def __init__(self):
        lat = lax.axis_index("lat")
        lon = lax.axis_index("lon")
        self.lat, self.lon = lat, lon
        self.z = lat // 8
        self.xlo = (lat // 4) % 2
        self.y = lat % 4
        self.xhi = lon // 2
        self.core = lon % 2
        self.x = self.xhi * 2 + self.xlo

    def at(self, x=None, y=None, z=None, core=None):
        x = self.x if x is None else x
        y = self.y if y is None else y
        z = self.z if z is None else z
        core = self.core if core is None else core
        return ((z * 2 + x % 2) * 4 + y, (x // 2) * 2 + core)


class Gather:
    def __init__(self, place, g, full, send, recv):
        p = place
        self.p, self.g, self.full, self.send, self.recv = p, g, full, send, recv
        self.up = p.at(y=(p.y + 1) % 4)
        self.down = p.at(y=(p.y + 3) % 4)
        self.east = p.at(x=(p.x + 1) % 4)
        self.west = p.at(x=(p.x + 3) % 4)
        self.twin = p.at(core=1 - p.core)
        self.partners = [p.at(z=(p.z + d) % 8) for d in range(1, 8)] + [
            self.up, self.down, self.east, self.west, self.twin, p.at(y=(p.y + 2) % 4)]
        self.sent = []

    def copy(self, slot, part, to):
        return pltpu.make_async_remote_copy(
            src_ref=part, dst_ref=part, send_sem=self.send.at[self.g, slot],
            recv_sem=self.recv.at[self.g, slot], device_id=to, device_id_type=MESH)

    def part(self, half, zs, line):
        return self.full.at[half, zs, line]

    def move(self, slot, to, zs, line):
        c = self.copy(slot, self.part(self.p.core, zs, line), to)
        c.start()
        self.sent.append(c)

    def landed(self, slot, zs, line, half=None):
        self.copy(slot, self.part(self.p.core if half is None else half, zs, line), self.twin).wait_recv()

    def line(self, other, dy):
        xlo = 1 - self.p.xlo if other else self.p.xlo
        return xlo * 4 + (self.p.y + dy) % 4

    def drain(self):
        for c in self.sent:
            c.wait_send()

    whole = pl.ds(0, 8)
    parts = (pl.ds(0, 4), pl.ds(4, 4))

    def start(self):
        p = self.p
        for d in range(1, 8):
            self.move(ZS + d - 1, p.at(z=(p.z + d) % 8), p.z, self.line(0, 0))

    def z_landed(self):
        p = self.p
        for d in range(1, 8):
            self.landed(ZS + d - 1, (p.z + 8 - d) % 8, self.line(0, 0))

    def after_z(self):
        self.z_landed()
        own = self.line(0, 0)
        self.move(YS + 0, self.up, self.whole, own)
        self.move(YS + 1, self.down, self.whole, own)
        self.to_x(0, 0)
        self.to_x(0, 1)
        self.move(SS + 0, self.twin, self.whole, own)

    def to_x(self, dy, part):
        self.move(XS + 2 * dy + part, (self.east, self.west)[part], self.parts[part], self.line(0, dy))

    def after_y(self):
        below, above = self.line(0, 3), self.line(0, 1)
        self.landed(YS + 0, self.whole, below)
        self.move(YS + 2, self.up, self.parts[0], below)
        self.landed(YS + 1, self.whole, above)
        self.move(YS + 3, self.down, self.parts[1], above)
        for dy in (3, 1):
            for part in (0, 1):
                self.to_x(dy, part)
        self.move(SS + 1, self.twin, self.whole, below)
        self.move(SS + 2, self.twin, self.whole, above)

    def after_far(self):
        for part in (0, 1):
            self.landed(YS + 2 + part, self.parts[part], self.line(0, 2))
            self.to_x(2, part)
            self.move(SS + 3 + part, self.twin, self.parts[part], self.line(0, 2))

    def after_x(self):
        for dy in (0, 3, 1, 2):
            for part in (0, 1):
                self.landed(XS + 2 * dy + part, self.parts[part], self.line(1, dy))
                self.move(SS + 5 + 2 * dy + part, self.twin, self.parts[part], self.line(1, dy))

    def finish(self):
        half = 1 - self.p.core
        self.landed(SS + 0, self.whole, self.line(0, 0), half)
        self.landed(SS + 1, self.whole, self.line(0, 3), half)
        self.landed(SS + 2, self.whole, self.line(0, 1), half)
        for part in (0, 1):
            self.landed(SS + 3 + part, self.parts[part], self.line(0, 2), half)
            for dy in range(4):
                self.landed(SS + 5 + 2 * dy + part, self.parts[part], self.line(1, dy), half)


class GatherZXY(Gather):
    def after_z(self):
        self.z_landed()
        own = self.line(0, 0)
        self.to_x(0, 0)
        self.to_x(0, 1)
        self.move(YS + 0, self.up, self.whole, own)
        self.move(YS + 1, self.down, self.whole, own)
        self.move(SS + 0, self.twin, self.whole, own)

    def after_x(self):
        other = self.line(1, 0)
        for part in (0, 1):
            self.landed(XS + part, self.parts[part], other)
        self.move(YS + 4, self.up, self.whole, other)
        self.move(YS + 5, self.down, self.whole, other)
        self.move(SS + 5, self.twin, self.whole, other)

    def after_y(self):
        for k in (0, 1):
            below, above = self.line(k, 3), self.line(k, 1)
            self.landed(YS + 4 * k, self.whole, below)
            self.move(YS + 4 * k + 2, self.up, self.parts[0], below)
            self.landed(YS + 4 * k + 1, self.whole, above)
            self.move(YS + 4 * k + 3, self.down, self.parts[1], above)
            self.move(SS + 5 * k + 1, self.twin, self.whole, below)
            self.move(SS + 5 * k + 2, self.twin, self.whole, above)

    def after_far(self):
        for k in (0, 1):
            for part in (0, 1):
                self.landed(YS + 4 * k + 2 + part, self.parts[part], self.line(k, 2))
                self.move(SS + 5 * k + 3 + part, self.twin, self.parts[part], self.line(k, 2))

    def finish(self):
        half = 1 - self.p.core
        for k in (0, 1):
            self.landed(SS + 5 * k, self.whole, self.line(k, 0), half)
            self.landed(SS + 5 * k + 1, self.whole, self.line(k, 3), half)
            self.landed(SS + 5 * k + 2, self.whole, self.line(k, 1), half)
            for part in (0, 1):
                self.landed(SS + 5 * k + 3 + part, self.parts[part], self.line(k, 2), half)


class GatherXYZ(Gather):
    def quarter(self, part):
        depth = self.full.shape[-1] // 2
        return pl.ds(0, self.full.shape[-2]), pl.ds(part * depth, depth)

    def start(self):
        p = self.p
        for part in (0, 1):
            mine = self.full.at[p.core, p.z, self.line(0, 0)].at[self.quarter(part)]
            c = self.copy(XS + part, mine, (self.east, self.west)[part])
            c.start()
            self.sent.append(c)

    def after_x(self):
        p = self.p
        for part in (0, 1):
            other = self.full.at[p.core, p.z, self.line(1, 0)].at[self.quarter(part)]
            self.copy(XS + part, other, self.twin).wait_recv()
        for k in (0, 1):
            for d in range(1, 4):
                self.move(YS + 3 * k + d - 1, p.at(y=(p.y + d) % 4), p.z, self.line(k, 0))

    def after_y(self):
        p = self.p
        for k in (0, 1):
            for d in range(1, 4):
                self.landed(YS + 3 * k + d - 1, p.z, self.line(k, 4 - d))
        for d in range(1, 8):
            self.move(ZS + d - 1, p.at(z=(p.z + d) % 8), p.z, self.whole)
        self.move(SS + 0, self.twin, p.z, self.whole)

    def after_z(self):
        p = self.p
        for d in range(1, 8):
            self.landed(ZS + d - 1, (p.z + 8 - d) % 8, self.whole)
            self.move(SS + d, self.twin, (p.z + 8 - d) % 8, self.whole)

    def finish(self):
        p = self.p
        for d in range(8):
            self.landed(SS + d, (p.z + 8 - d) % 8, self.whole, 1 - p.core)


def times(a, b):
    return lax.dot_general(a, b, NT, preferred_element_type=jnp.float32)


def norm_groups(parts, gain):
    width = 128 * len(parts)
    mean = jnp.sum(sum(parts), -1, keepdims=True) / width
    parts = [p - mean for p in parts]
    spread = jnp.sum(sum(p * p for p in parts), -1, keepdims=True) / width
    scale = lax.rsqrt(spread + 1e-05)
    return [p * scale * gain[:, 128 * k:128 * k + 128] for k, p in enumerate(parts)]


def prepare_bias(flat, table, heads):
    lane = lax.broadcasted_iota(jnp.int32, (8, 128), 1)

    def eight(i, _):
        t, q = i // 18, i % 18
        rows = pl.ds(pl.multiple_of(t * 8, 8), 8)
        block = flat[rows, pl.ds(pl.multiple_of(q * 1152, 128), 1152)] * LOG2E
        for s in range(8):
            first, second = block[:, 128 * s:128 * s + 128], block[:, 128 * s + 128:128 * s + 256]
            if s:
                first, second = pltpu.roll(first, 128 - 16 * s, 1), pltpu.roll(second, 128 - 16 * s, 1)
                first = jnp.where(lane < 128 - 16 * s, first, second)
            second = jnp.where(lane < 16, second, ABSENT)
            where = pl.ds(t * 8 * WT + q * 8 + s, 8, stride=WT)
            table[0, where, :] = first
            table[1, where, :] = second
        return 0

    lax.fori_loop(0, heads // 8 * 18, eight, 0)


def attend(q, k, v, bias0, bias1, mask):
    lane = lax.broadcasted_iota(jnp.int32, (WT, 128), 1) // 32
    none = jnp.zeros((256 - WT, 128), jnp.bfloat16)
    heads = jnp.concatenate([jnp.where(lane == h, q, jnp.zeros_like(q)) for h in range(4)], 0)
    scores = times(heads, jnp.concatenate([k, none], 0)) * (LOG2E / 32 ** 0.5)
    bias = jnp.concatenate([bias0, bias1], 1)
    scores = scores + bias + jnp.concatenate([mask] * 4, 0)
    top = jnp.max(scores, -1, keepdims=True)
    weights = jnp.exp2(scores - top).astype(jnp.bfloat16)
    values = jnp.concatenate([jnp.concatenate([v, none], 0), jnp.ones((256, 128), jnp.bfloat16)], 1)
    mixed = jnp.dot(weights, values, preferred_element_type=jnp.float32)
    total, over = mixed[:WT, :128], mixed[:WT, 128:]
    for h in range(1, 4):
        total = jnp.where(lane == h, mixed[WT * h:WT * h + WT, :128], total)
        over = jnp.where(lane == h, mixed[WT * h:WT * h + WT, 128:], over)
    return total / over


def loop(count, step, first=0):
    lax.fori_loop(first, count, lambda i, c: (step(i), c)[1], 0)


def block_kernel(
    tok, land, surface, table, levels, gain1, wqkv1, wout1, gain_merge, wmerge, gain2, wqkv2, wout2,
    bias1_hbm, bias2_hbm,
    one, two,
    emb,
    full0, full1, full2, full3, flat1, flat2, table1, table2, mask,
    e1, first1, south1, rw1, rn1, rc1, bw1, bn1, bc1, qw, ow, x1, qkv1, s1, mg, mn,
    s2, e2, first2, south2, rw2, rn2, rc2, bw2, bn2, bc2, x2, qkv2,
    sw1, sn1, sc1, sw2, sn2, sc2,
    send, recv, hsend, hrecv, local,
):
    p = Place()
    full = (full0, full1, full2, full3)
    kinds = (Gather, Gather, Gather, Gather)
    n0, n1, n2, n3 = nets = [kinds[g](p, g, full[g], send, recv) for g in range(NG)]
    north, south = (p.lat + 63) % 64, (p.lat + 1) % 64
    west, east = (p.lon + 3) % 4, (p.lon + 1) % 4
    around = [(p.lat, west), (north, p.lon), (north, west), (p.lat, east), (south, p.lon), (south, east)]
    partners = n0.partners + around
    barrier = pltpu.get_barrier_semaphore()
    for to in partners:
        pl.semaphore_signal(barrier, inc=1, device_id=to, device_id_type=MESH)
    b1 = pltpu.make_async_copy(bias1_hbm, flat1, local.at[0])
    b2 = pltpu.make_async_copy(bias2_hbm, flat2, local.at[1])
    b1.start()
    b2.start()

    own = n0.line(0, 0)

    def halved(w):
        depth = w.shape[1] // 2
        return w[:, pl.ds(pl.multiple_of(p.core * depth, depth), depth)]

    full0[p.core, p.z, own] = jnp.concatenate(
        [halved(wqkv1).astype(jnp.float32), halved(wout1).astype(jnp.float32)], 0).astype(jnp.bfloat16)
    full1[p.core, p.z, own] = halved(wmerge)
    full2[p.core, p.z, own] = halved(wqkv2)
    full3[p.core, p.z, own] = halved(wout2)
    pl.semaphore_wait(barrier, len(partners))

    def neighbour(slot, src, dst, way):
        return pltpu.make_async_remote_copy(
            src_ref=src, dst_ref=dst, send_sem=hsend.at[slot], recv_sem=hrecv.at[slot],
            device_id=around[way], device_id_type=MESH)


    n0.start()
    n1.start()
    sixteen = lax.broadcasted_iota(jnp.int32, (16, 512), 0)
    sixteen2 = lax.broadcasted_iota(jnp.int32, (16, 1024), 0)

    numbers = lax.broadcasted_iota(jnp.int32, levels.shape, 0)
    rows = [jnp.sum(jnp.where(numbers == table[i], levels[...], 0.0), 0, keepdims=True) for i in range(2)]
    level = jnp.where(lax.broadcasted_iota(jnp.int32, (48, 512), 0) % 2 == 0, rows[0], rows[1])
    patch = lax.broadcasted_iota(jnp.int32, (48, 24), 0) // 2 == lax.broadcasted_iota(jnp.int32, (48, 24), 1)

    def row_norm(r):
        kinds = land[pl.ds(r, 1), :].astype(jnp.float32)
        kind = jnp.sum(jnp.where(patch, kinds, 0.0), -1, keepdims=True)
        ground = jnp.where(kind == 0.0, surface[0:1, :], jnp.where(kind == 1.0, surface[1:2, :], surface[2:3, :]))
        v = tok[pl.ds(r * 24, 24)].astype(jnp.float32).reshape(48, 512) + ground + level
        emb[pl.ds(pl.multiple_of(r * 48, 16), 48), :] = v
        n = norm_groups([v[:, 128 * k:128 * k + 128] for k in range(4)], gain1[...])
        e1[r, 0:8, :] = jnp.zeros((8, 512), jnp.float32)
        e1[r, 48:64, :] = jnp.zeros((16, 512), jnp.float32)
        for k in range(4):
            e1[r, 4:52, 128 * k:128 * k + 128] = n[k]
        first1[r] = e1[r, 0:16, :].astype(jnp.bfloat16)

    loop(12, row_norm)
    for r in range(3):
        south1[r] = e1[r, 16:64, :].astype(jnp.bfloat16)
    halo1 = [neighbour(0, first1.at[pl.ds(3, 9)], rw1, 0), neighbour(1, south1, rn1, 1),
             neighbour(2, first1.at[pl.ds(0, 3)], rc1, 2)]
    for c in halo1:
        c.start()

    n0.after_z()
    n2.start()
    half = lambda axis: lax.broadcasted_iota(jnp.int32, (WT, 256), axis) >= WT // 2
    cut = (half(0) != half(1)) & (p.lat == 63)
    mask[0] = jnp.zeros((WT, 256), jnp.float32)
    mask[1] = jnp.where(cut, ABSENT, 0.0)
    b1.wait()
    prepare_bias(flat1, table1, 16)
    n0.after_y()
    n1.after_z()
    b2.wait()
    prepare_bias(flat2, table2, 32)

    n0.after_far()
    n2.after_z()
    n0.after_x()
    for c in halo1:
        c.wait_recv()

    def take_west(r):
        e1[r + 3, 48:64, :] = jnp.where(sixteen >= 4, rw1[r].astype(jnp.float32), e1[r + 3, 48:64, :])

    loop(9, take_west)
    for r in range(3):
        n = rn1[r].astype(jnp.float32)
        e1[12 + r, 16:48, :] = n[:32]
        e1[12 + r, 48:64, :] = jnp.where(sixteen >= 4, rc1[r].astype(jnp.float32), n[32:])
    for w in range(4):
        a, b = w // 2, w % 2
        x1[WT * w:WT * w + WT, :] = e1[3 + 6 * a:9 + 6 * a, 16 + 24 * b:40 + 24 * b, :].reshape(
            WT, 512).astype(jnp.bfloat16)


    n1.after_y()
    n0.finish()
    def unpack(i):
        z, l = i // 4, 2 * (i % 4)
        both = [jnp.concatenate([full0[0, z, l + d], full0[1, z, l + d]], 1).astype(jnp.float32)
                for d in range(2)]
        qw[pl.ds(pl.multiple_of(48 * i, 16), 48), :] = jnp.concatenate(
            [both[0][:24], both[1][:24]], 0).astype(jnp.bfloat16)
        ow[pl.ds(pl.multiple_of(16 * i, 16), 16), :] = jnp.concatenate(
            [both[0][24:], both[1][24:]], 0).astype(jnp.bfloat16)

    loop(32, unpack)

    def project1(n):
        out = times(x1[...], qw[pl.ds(pl.multiple_of(256 * n, 256), 256), :]).astype(jnp.bfloat16)
        qkv1[2 * n] = out[:, :128]
        qkv1[2 * n + 1] = out[:, 128:]

    loop(6, project1)

    def attend1(i):
        w, g = 3 - i // 4, i % 4
        rows = pl.ds(pl.multiple_of(WT * w, 16), WT)
        heads = pl.ds(pl.multiple_of(4 * WT * g, 16), 4 * WT)
        out = attend(qkv1[g, rows, :], qkv1[4 + g, rows, :], qkv1[8 + g, rows, :],
                     table1[0, heads, :], table1[1, heads, :], mask[w // 2])
        e1[pl.ds(3 + 6 * (w // 2), 6), pl.ds(pl.multiple_of(16 + 24 * (w % 2), 8), 24),
           pl.ds(pl.multiple_of(128 * g, 128), 128)] = out.reshape(6, 24, 128)

    loop(8, attend1)
    for r in range(3):
        bn1[r] = e1[12 + r, 16:64, :].astype(jnp.bfloat16)
        bc1[r] = e1[12 + r, 48:64, :].astype(jnp.bfloat16)
    back1 = [neighbour(3, bn1, sn1, 4), neighbour(4, bc1, sc1, 5)]
    for c in back1:
        c.start()
    loop(12, attend1, 8)

    def last_columns(r):
        bw1[r] = e1[r + 3, 48:64, :].astype(jnp.bfloat16)

    loop(9, last_columns)
    back1.append(neighbour(5, bw1, sw1, 3))
    back1[2].start()
    n3.start()
    n1.after_far()
    n2.after_y()
    loop(16, attend1, 12)
    n1.after_x()
    n3.after_z()
    for c in back1:
        c.wait_recv()

    def keep_west(r):
        e1[r + 3, 0:16, :] = jnp.where(sixteen >= 4, sw1[r].astype(jnp.float32), e1[r + 3, 0:16, :])

    loop(9, keep_west)
    for r in range(3):
        e1[r, 16:64, :] = sn1[r].astype(jnp.float32)
        e1[r, 0:16, :] = sc1[r].astype(jnp.float32)

    def collect1(r):
        x1[pl.ds(pl.multiple_of(48 * r, 16), 48), :] = e1[r, 4:52, :].astype(jnp.bfloat16)

    loop(12, collect1)
    for n in range(2):
        cols = slice(256 * n, 256 * n + 256)
        out = emb[:, cols] + times(x1[...], ow[cols, :])
        one[:, :, cols] = out.reshape(288, 2, 256).astype(jnp.bfloat16)
        s1[2 * n] = out[:, :128]
        s1[2 * n + 1] = out[:, 128:]

    def merge_rows(i):
        for dr in range(2):
            for dc in range(2):
                for level in range(2):
                    for k in range(4):
                        mg[(dc * 2 + dr) * 4 + k, pl.ds(24 * i + level, 12, stride=2), :] = s1[
                            k, pl.ds((2 * i + dr) * 48 + 2 * dc + level, 12, stride=4), :]

    loop(6, merge_rows)

    def merge_norm(c):
        rows = pl.ds(pl.multiple_of(16 * c, 16), 16)
        n = norm_groups([mg[k, rows, :] for k in range(16)], gain_merge[...])
        for k in range(16):
            mn[rows, 128 * k:128 * k + 128] = n[k].astype(jnp.bfloat16)

    loop(9, merge_norm)

    n1.finish()
    def merge_product(n):
        zs = pl.ds(2 * n, 2)
        out = times(mn[:, :1024], full1[0, zs].reshape(256, 1024))
        out = out + times(mn[:, 1024:], full1[1, zs].reshape(256, 1024))
        s2[2 * n] = out[:, :128]
        s2[2 * n + 1] = out[:, 128:]

    loop(4, merge_product)

    n2.after_far()
    def row_norm2(r):
        rows = pl.ds(pl.multiple_of(24 * r, 8), 24)
        n = norm_groups([s2[k, rows, :] for k in range(8)], gain2[...])
        e2[r, 0:8, :] = jnp.zeros((8, 1024), jnp.float32)
        e2[r, 24:40, :] = jnp.zeros((16, 1024), jnp.float32)
        for k in range(8):
            e2[r, 4:28, 128 * k:128 * k + 128] = n[k]
        first2[r] = e2[r, 0:16, :].astype(jnp.bfloat16)
        south2[r] = e2[r, 16:32, :].astype(jnp.bfloat16)

    loop(6, row_norm2)
    halo2 = [neighbour(6, first2.at[pl.ds(3, 3)], rw2, 0), neighbour(7, south2.at[pl.ds(0, 3)], rn2, 1),
             neighbour(8, first2.at[pl.ds(0, 3)], rc2, 2)]
    for c in halo2:
        c.start()
    n2.after_x()
    for c in halo2:
        c.wait_recv()
    for r in range(3):
        e2[3 + r, 24:40, :] = jnp.where(sixteen2 >= 4, rw2[r].astype(jnp.float32), e2[3 + r, 24:40, :])
        e2[6 + r, 16:32, :] = rn2[r].astype(jnp.float32)
        e2[6 + r, 24:40, :] = jnp.where(sixteen2 >= 4, rc2[r].astype(jnp.float32), e2[6 + r, 24:40, :])
    x2[...] = e2[3:9, 16:40, :].reshape(WT, 1024).astype(jnp.bfloat16)


    n2.finish()
    n3.after_y()
    def project2(z):
        first, second = [full2[h, z].reshape(384, 512) for h in range(2)]
        out = (times(x2[:, :512], first) + times(x2[:, 512:], second)).astype(jnp.bfloat16)
        for k in range(3):
            qkv2[3 * z + k] = out[:, 128 * k:128 * k + 128]

    loop(8, project2)

    def attend2(g):
        heads = pl.ds(pl.multiple_of(4 * WT * g, 16), 4 * WT)
        out = attend(qkv2[g], qkv2[8 + g], qkv2[16 + g], table2[0, heads, :], table2[1, heads, :], mask[1])
        e2[3:9, 16:40, pl.ds(pl.multiple_of(128 * g, 128), 128)] = out.reshape(6, 24, 128)

    n3.after_far()
    back2 = []
    for h in range(2):
        loop(4 * h + 4, attend2, 4 * h)
        cols = slice(512 * h, 512 * h + 512)
        for r in range(3):
            bw2[h, r] = e2[3 + r, 24:40, cols].astype(jnp.bfloat16)
            bn2[h, r] = e2[6 + r, 16:32, cols].astype(jnp.bfloat16)
            bc2[h, r] = e2[6 + r, 24:40, cols].astype(jnp.bfloat16)
        some = [neighbour(9 + 3 * h, bw2.at[h], sw2.at[h], 3), neighbour(10 + 3 * h, bn2.at[h], sn2.at[h], 4),
                neighbour(11 + 3 * h, bc2.at[h], sc2.at[h], 5)]
        for c in some:
            c.start()
        if h == 0:
            n3.after_x()
        back2 += some
    n3.finish()
    for c in back2:
        c.wait_recv()
    for h in range(2):
        cols = slice(512 * h, 512 * h + 512)
        for r in range(3):
            e2[3 + r, 0:16, cols] = jnp.where(sixteen >= 4, sw2[h, r].astype(jnp.float32), e2[3 + r, 0:16, cols])
            e2[r, 16:32, cols] = sn2[h, r].astype(jnp.float32)
            e2[r, 0:16, cols] = sc2[h, r].astype(jnp.float32)
    for r in range(6):
        x2[24 * r:24 * r + 24, :] = e2[r, 4:28, :].astype(jnp.bfloat16)

    def last(n):
        zs = pl.ds(2 * n, 2)
        out = times(x2[:, :512], full3[0, zs].reshape(256, 512))
        out = out + times(x2[:, 512:], full3[1, zs].reshape(256, 512))
        out = out + jnp.concatenate([s2[2 * n], s2[2 * n + 1]], 1)
        two[:, pl.ds(pl.multiple_of(256 * n, 256), 256)] = out.astype(jnp.bfloat16)

    loop(4, last)
    for c in halo1 + back1 + halo2 + back2:
        c.wait_send()
    for net in nets:
        net.drain()


def shards(
    tokens, land_sea, surface_embed, level_table, level_embed, gain1, w_qkv1, bias1, w_out1,
    gain_merge, w_merge, gain2, w_qkv2, bias2, w_out2,
):
    f32, bf16 = jnp.float32, jnp.bfloat16
    shapes = [(2, 8, 8, rows, depth // 2) for rows, depth in GROUPS]
    scratch = [pltpu.VMEM((576, 512), f32)] + [pltpu.VMEM(s, bf16) for s in shapes] + [pltpu.VMEM(s, t) for s, t in (
        ((16, WT * WT), f32), ((32, WT * WT), f32),
        ((2, 16 * WT, 128), f32), ((2, 32 * WT, 128), f32), ((2, WT, 256), f32),
        ((15, 64, 512), f32), ((12, 16, 512), bf16), ((3, 48, 512), bf16),
        ((9, 16, 512), bf16), ((3, 48, 512), bf16), ((3, 16, 512), bf16),
        ((9, 16, 512), bf16), ((3, 48, 512), bf16), ((3, 16, 512), bf16),
        ((1536, 512), bf16), ((512, 512), bf16), ((576, 512), bf16), ((12, 576, 128), bf16),
        ((4, 576, 128), f32), ((16, WT, 128), f32), ((WT, 2048), bf16),
        ((8, WT, 128), f32), ((9, 40, 1024), f32), ((6, 16, 1024), bf16), ((6, 16, 1024), bf16),
        ((3, 16, 1024), bf16), ((3, 16, 1024), bf16), ((3, 16, 1024), bf16),
        ((2, 3, 16, 512), bf16), ((2, 3, 16, 512), bf16), ((2, 3, 16, 512), bf16),
        ((WT, 1024), bf16), ((24, WT, 128), bf16),
        ((9, 16, 512), bf16), ((3, 48, 512), bf16), ((3, 16, 512), bf16),
        ((2, 3, 16, 512), bf16), ((2, 3, 16, 512), bf16), ((2, 3, 16, 512), bf16),
    )] + [
        pltpu.SemaphoreType.DMA((NG, SLOTS)), pltpu.SemaphoreType.DMA((NG, SLOTS)),
        pltpu.SemaphoreType.DMA((15,)), pltpu.SemaphoreType.DMA((15,)), pltpu.SemaphoreType.DMA((2,)),
    ]
    vmem, anywhere = pl.BlockSpec(memory_space=pltpu.VMEM), pl.BlockSpec(memory_space=pl.ANY)
    one, two = pl.pallas_call(
        block_kernel,
        out_shape=[jax.ShapeDtypeStruct((288, 2, 512), bf16), jax.ShapeDtypeStruct((WT, 1024), bf16)],
        in_specs=[vmem] * 3 + [pl.BlockSpec(memory_space=pltpu.SMEM)] + [vmem] * 9 + [anywhere] * 2,
        out_specs=[vmem] * 2,
        scratch_shapes=scratch,
        compiler_params=pltpu.CompilerParams(
            collective_id=0, has_side_effects=True, vmem_limit_bytes=60 * 2**20),
    )(tokens.reshape(288, 2, 512), land_sea, surface_embed, level_table, level_embed, gain1[None], w_qkv1.T,
      w_out1.T, gain_merge[None], w_merge.T, gain2[None], w_qkv2.T, w_out2.T, bias1, bias2)
    return one.reshape(12, 24, 2, 512), two.reshape(6, 12, 2, 1024)


def solution(mesh):
    placed = (
        P("lat", "lon", None, None), P("lat", "lon"), P(), P(), P(), P(),
        P(None, "lat"), P(), P(None, "lat"), P(), P(None, "lat"), P(), P(None, "lat"), P(), P(None, "lat"),
    )
    return jax.shard_map(
        shards,
        mesh=mesh,
        in_specs=placed,
        out_specs=(P("lat", "lon", None, None), P("lat", "lon", None, None)),
        check_vma=False,
    )
```

```python
import jax
import jax.numpy as jnp
from jax import lax
from jax.experimental import pallas as pl
from jax.experimental.pallas import tpu as pltpu
from jax.sharding import PartitionSpec as P

WT = 144
NT = (((1,), (1,)), ((), ()))
LOG2E = 1.4426950408889634
ABSENT = -1e30
MESH = pl.DeviceIdType.MESH
GROUPS = ((32, 512), (16, 2048), (48, 1024), (16, 1024))
NG = len(GROUPS)
ZS, YS, XS, SS = 0, 7, 15, 23
SLOTS = 36


class Place:
    def __init__(self):
        lat = lax.axis_index("lat")
        lon = lax.axis_index("lon")
        self.lat, self.lon = lat, lon
        self.z = lat // 8
        self.xlo = (lat // 4) % 2
        self.y = lat % 4
        self.xhi = lon // 2
        self.core = lon % 2
        self.x = self.xhi * 2 + self.xlo

    def at(self, x=None, y=None, z=None, core=None):
        x = self.x if x is None else x
        y = self.y if y is None else y
        z = self.z if z is None else z
        core = self.core if core is None else core
        return ((z * 2 + x % 2) * 4 + y, (x // 2) * 2 + core)


class Gather:
    def __init__(self, place, g, full, send, recv):
        p = place
        self.p, self.g, self.full, self.send, self.recv = p, g, full, send, recv
        self.up = p.at(y=(p.y + 1) % 4)
        self.down = p.at(y=(p.y + 3) % 4)
        self.east = p.at(x=(p.x + 1) % 4)
        self.west = p.at(x=(p.x + 3) % 4)
        self.twin = p.at(core=1 - p.core)
        self.partners = [p.at(z=(p.z + d) % 8) for d in range(1, 8)] + [
            self.up, self.down, self.east, self.west, self.twin, p.at(y=(p.y + 2) % 4)]
        self.sent = []

    def copy(self, slot, part, to):
        return pltpu.make_async_remote_copy(
            src_ref=part, dst_ref=part, send_sem=self.send.at[self.g, slot],
            recv_sem=self.recv.at[self.g, slot], device_id=to, device_id_type=MESH)

    def part(self, half, zs, line):
        return self.full.at[half, zs, line]

    def move(self, slot, to, zs, line):
        c = self.copy(slot, self.part(self.p.core, zs, line), to)
        c.start()
        self.sent.append(c)

    def landed(self, slot, zs, line, half=None):
        self.copy(slot, self.part(self.p.core if half is None else half, zs, line), self.twin).wait_recv()

    def line(self, other, dy):
        xlo = 1 - self.p.xlo if other else self.p.xlo
        return xlo * 4 + (self.p.y + dy) % 4

    def drain(self):
        for c in self.sent:
            c.wait_send()

    whole = pl.ds(0, 8)
    parts = (pl.ds(0, 4), pl.ds(4, 4))

    def start(self):
        p = self.p
        for d in range(1, 8):
            self.move(ZS + d - 1, p.at(z=(p.z + d) % 8), p.z, self.line(0, 0))

    def z_landed(self):
        p = self.p
        for d in range(1, 8):
            self.landed(ZS + d - 1, (p.z + 8 - d) % 8, self.line(0, 0))

    def after_z(self):
        self.z_landed()
        own = self.line(0, 0)
        self.move(YS + 0, self.up, self.whole, own)
        self.move(YS + 1, self.down, self.whole, own)
        self.to_x(0, 0)
        self.to_x(0, 1)
        self.move(SS + 0, self.twin, self.whole, own)

    def to_x(self, dy, part):
        self.move(XS + 2 * dy + part, (self.east, self.west)[part], self.parts[part], self.line(0, dy))

    def after_y(self):
        below, above = self.line(0, 3), self.line(0, 1)
        self.landed(YS + 0, self.whole, below)
        self.move(YS + 2, self.up, self.parts[0], below)
        self.landed(YS + 1, self.whole, above)
        self.move(YS + 3, self.down, self.parts[1], above)
        for dy in (3, 1):
            for part in (0, 1):
                self.to_x(dy, part)
        self.move(SS + 1, self.twin, self.whole, below)
        self.move(SS + 2, self.twin, self.whole, above)

    def after_far(self):
        for part in (0, 1):
            self.landed(YS + 2 + part, self.parts[part], self.line(0, 2))
            self.to_x(2, part)
            self.move(SS + 3 + part, self.twin, self.parts[part], self.line(0, 2))

    def after_x(self):
        for dy in (0, 3, 1, 2):
            for part in (0, 1):
                self.landed(XS + 2 * dy + part, self.parts[part], self.line(1, dy))
                self.move(SS + 5 + 2 * dy + part, self.twin, self.parts[part], self.line(1, dy))

    def finish(self):
        half = 1 - self.p.core
        self.landed(SS + 0, self.whole, self.line(0, 0), half)
        self.landed(SS + 1, self.whole, self.line(0, 3), half)
        self.landed(SS + 2, self.whole, self.line(0, 1), half)
        for part in (0, 1):
            self.landed(SS + 3 + part, self.parts[part], self.line(0, 2), half)
            for dy in range(4):
                self.landed(SS + 5 + 2 * dy + part, self.parts[part], self.line(1, dy), half)


class GatherZXY(Gather):
    def after_z(self):
        self.z_landed()
        own = self.line(0, 0)
        self.to_x(0, 0)
        self.to_x(0, 1)
        self.move(YS + 0, self.up, self.whole, own)
        self.move(YS + 1, self.down, self.whole, own)
        self.move(SS + 0, self.twin, self.whole, own)

    def after_x(self):
        other = self.line(1, 0)
        for part in (0, 1):
            self.landed(XS + part, self.parts[part], other)
        self.move(YS + 4, self.up, self.whole, other)
        self.move(YS + 5, self.down, self.whole, other)
        self.move(SS + 5, self.twin, self.whole, other)

    def after_y(self):
        for k in (0, 1):
            below, above = self.line(k, 3), self.line(k, 1)
            self.landed(YS + 4 * k, self.whole, below)
            self.move(YS + 4 * k + 2, self.up, self.parts[0], below)
            self.landed(YS + 4 * k + 1, self.whole, above)
            self.move(YS + 4 * k + 3, self.down, self.parts[1], above)
            self.move(SS + 5 * k + 1, self.twin, self.whole, below)
            self.move(SS + 5 * k + 2, self.twin, self.whole, above)

    def after_far(self):
        for k in (0, 1):
            for part in (0, 1):
                self.landed(YS + 4 * k + 2 + part, self.parts[part], self.line(k, 2))
                self.move(SS + 5 * k + 3 + part, self.twin, self.parts[part], self.line(k, 2))

    def finish(self):
        half = 1 - self.p.core
        for k in (0, 1):
            self.landed(SS + 5 * k, self.whole, self.line(k, 0), half)
            self.landed(SS + 5 * k + 1, self.whole, self.line(k, 3), half)
            self.landed(SS + 5 * k + 2, self.whole, self.line(k, 1), half)
            for part in (0, 1):
                self.landed(SS + 5 * k + 3 + part, self.parts[part], self.line(k, 2), half)


class GatherXYZ(Gather):
    def quarter(self, part):
        depth = self.full.shape[-1] // 2
        return pl.ds(0, self.full.shape[-2]), pl.ds(part * depth, depth)

    def start(self):
        p = self.p
        for part in (0, 1):
            mine = self.full.at[p.core, p.z, self.line(0, 0)].at[self.quarter(part)]
            c = self.copy(XS + part, mine, (self.east, self.west)[part])
            c.start()
            self.sent.append(c)

    def after_x(self):
        p = self.p
        for part in (0, 1):
            other = self.full.at[p.core, p.z, self.line(1, 0)].at[self.quarter(part)]
            self.copy(XS + part, other, self.twin).wait_recv()
        for k in (0, 1):
            for d in range(1, 4):
                self.move(YS + 3 * k + d - 1, p.at(y=(p.y + d) % 4), p.z, self.line(k, 0))

    def after_y(self):
        p = self.p
        for k in (0, 1):
            for d in range(1, 4):
                self.landed(YS + 3 * k + d - 1, p.z, self.line(k, 4 - d))
        for d in range(1, 8):
            self.move(ZS + d - 1, p.at(z=(p.z + d) % 8), p.z, self.whole)
        self.move(SS + 0, self.twin, p.z, self.whole)

    def after_z(self):
        p = self.p
        for d in range(1, 8):
            self.landed(ZS + d - 1, (p.z + 8 - d) % 8, self.whole)
            self.move(SS + d, self.twin, (p.z + 8 - d) % 8, self.whole)

    def finish(self):
        p = self.p
        for d in range(8):
            self.landed(SS + d, (p.z + 8 - d) % 8, self.whole, 1 - p.core)


def times(a, b):
    return lax.dot_general(a, b, NT, preferred_element_type=jnp.float32)


def norm_groups(parts, gain):
    width = 128 * len(parts)
    mean = jnp.sum(sum(parts), -1, keepdims=True) / width
    parts = [p - mean for p in parts]
    spread = jnp.sum(sum(p * p for p in parts), -1, keepdims=True) / width
    scale = lax.rsqrt(spread + 1e-05)
    return [p * scale * gain[:, 128 * k:128 * k + 128] for k, p in enumerate(parts)]


def prepare_bias(flat, table, heads):
    lane = lax.broadcasted_iota(jnp.int32, (8, 128), 1)

    def eight(i, _):
        t, q = i // 18, i % 18
        rows = pl.ds(pl.multiple_of(t * 8, 8), 8)
        block = flat[rows, pl.ds(pl.multiple_of(q * 1152, 128), 1152)] * LOG2E
        for s in range(8):
            first, second = block[:, 128 * s:128 * s + 128], block[:, 128 * s + 128:128 * s + 256]
            if s:
                first, second = pltpu.roll(first, 128 - 16 * s, 1), pltpu.roll(second, 128 - 16 * s, 1)
                first = jnp.where(lane < 128 - 16 * s, first, second)
            second = jnp.where(lane < 16, second, ABSENT)
            where = pl.ds(t * 8 * WT + q * 8 + s, 8, stride=WT)
            table[0, where, :] = first
            table[1, where, :] = second
        return 0

    lax.fori_loop(0, heads // 8 * 18, eight, 0)


def attend(q, k, v, bias0, bias1, mask):
    lane = lax.broadcasted_iota(jnp.int32, (WT, 128), 1) // 32
    none = jnp.zeros((256 - WT, 128), jnp.bfloat16)
    heads = jnp.concatenate([jnp.where(lane == h, q, jnp.zeros_like(q)) for h in range(4)], 0)
    scores = times(heads, jnp.concatenate([k, none], 0)) * (LOG2E / 32 ** 0.5)
    bias = jnp.concatenate([bias0, bias1], 1)
    scores = scores + bias + jnp.concatenate([mask] * 4, 0)
    top = jnp.max(scores, -1, keepdims=True)
    weights = jnp.exp2(scores - top).astype(jnp.bfloat16)
    values = jnp.concatenate([jnp.concatenate([v, none], 0), jnp.ones((256, 128), jnp.bfloat16)], 1)
    mixed = jnp.dot(weights, values, preferred_element_type=jnp.float32)
    total, over = mixed[:WT, :128], mixed[:WT, 128:]
    for h in range(1, 4):
        total = jnp.where(lane == h, mixed[WT * h:WT * h + WT, :128], total)
        over = jnp.where(lane == h, mixed[WT * h:WT * h + WT, 128:], over)
    return total / over


def loop(count, step, first=0, unroll=1):
    lax.fori_loop(first, count, lambda i, c: (step(i), c)[1], 0, unroll=unroll)


def block_kernel(
    tok_hbm, land_hbm, surface_hbm, table, levels_hbm, gain1_hbm, wqkv1_hbm, wout1_hbm, gain_merge_hbm,
    wmerge_hbm, gain2_hbm, wqkv2_hbm, wout2_hbm, bias1_hbm, bias2_hbm,
    one, two,
    tok, land, surface, levels, gain1, wqkv1, wout1, gain_merge, wmerge, gain2, wqkv2, wout2,
    emb,
    full0, full1, full2, full3, flat1, flat2, table1, table2, mask,
    pad, e1, hw1, hn1, hc1, rw1, rn1, rc1, bw1, bn1, bc1, qw, ow, x1, qkv1, s1, mg, mn,
    s2, e2, hw2, hn2, hc2, rw2, rn2, rc2, bw2, bn2, bc2, x2, qkv2,
    sw1, sn1, sc1, sw2, sn2, sc2,
    send, recv, hsend, hrecv, local,
):
    p = Place()
    full = (full0, full1, full2, full3)
    kinds = (Gather, Gather, Gather, Gather)
    n0, n1, n2, n3 = nets = [kinds[g](p, g, full[g], send, recv) for g in range(NG)]
    north, south = (p.lat + 63) % 64, (p.lat + 1) % 64
    west, east = (p.lon + 3) % 4, (p.lon + 1) % 4
    around = [(p.lat, west), (north, p.lon), (north, west), (p.lat, east), (south, p.lon), (south, east)]
    partners = n0.partners + around
    barrier = pltpu.get_barrier_semaphore()
    for to in partners:
        pl.semaphore_signal(barrier, inc=1, device_id=to, device_id_type=MESH)
    pairs = (
        (wqkv1_hbm, wqkv1), (wout1_hbm, wout1), (tok_hbm, tok), (land_hbm, land), (surface_hbm, surface),
        (levels_hbm, levels), (gain1_hbm, gain1), (wmerge_hbm, wmerge), (wqkv2_hbm, wqkv2), (wout2_hbm, wout2),
        (gain_merge_hbm, gain_merge), (gain2_hbm, gain2))
    inputs = [pltpu.make_async_copy(src, dst, local.at[2 + i]) for i, (src, dst) in enumerate(pairs)]
    for c in inputs:
        c.start()
    b1 = pltpu.make_async_copy(bias1_hbm, flat1, local.at[0])
    b2 = pltpu.make_async_copy(bias2_hbm, flat2, local.at[1])
    b1.start()
    b2.start()

    for c in inputs:
        c.wait()

    own = n0.line(0, 0)

    def halved(w):
        depth = w.shape[1] // 2
        return w[:, pl.ds(pl.multiple_of(p.core * depth, depth), depth)]

    full0[p.core, p.z, own] = jnp.concatenate(
        [halved(wqkv1).astype(jnp.float32), halved(wout1).astype(jnp.float32)], 0).astype(jnp.bfloat16)
    full1[p.core, p.z, own] = halved(wmerge)
    full2[p.core, p.z, own] = halved(wqkv2)
    full3[p.core, p.z, own] = halved(wout2)
    pl.semaphore_wait(barrier, len(partners))

    def neighbour(slot, src, dst, way):
        return pltpu.make_async_remote_copy(
            src_ref=src, dst_ref=dst, send_sem=hsend.at[slot], recv_sem=hrecv.at[slot],
            device_id=around[way], device_id_type=MESH)


    n0.start()
    n1.start()
    n2.start()

    def pack(out, source, count, rows, first):
        for i, r in enumerate(rows):
            pad[count * i:count * i + count, :] = source[r, first:first + count, :]
        out[...] = pad[:out.shape[0], :].astype(jnp.bfloat16)

    def unpack_rows(target, came, count, rows, first):
        pad[:came.shape[0], :] = came[...].astype(jnp.float32)
        for i, r in enumerate(rows):
            target[r, first:first + count, :] = pad[count * i:count * i + count, :]

    pad[...] = jnp.zeros((112, 512), jnp.float32)
    own_rows, first_rows, next_rows = range(3, 12), range(3), range(12, 15)

    numbers = lax.broadcasted_iota(jnp.int32, levels.shape, 0)
    rows = [jnp.sum(jnp.where(numbers == table[i], levels[...], 0.0), 0, keepdims=True) for i in range(2)]
    level = jnp.where(lax.broadcasted_iota(jnp.int32, (48, 512), 0) % 2 == 0, rows[0], rows[1])
    patch = lax.broadcasted_iota(jnp.int32, (48, 24), 0) // 2 == lax.broadcasted_iota(jnp.int32, (48, 24), 1)

    def row_norm(r):
        kinds = land[pl.ds(r, 1), :].astype(jnp.float32)
        kind = jnp.sum(jnp.where(patch, kinds, 0.0), -1, keepdims=True)
        ground = jnp.where(kind == 0.0, surface[0:1, :], jnp.where(kind == 1.0, surface[1:2, :], surface[2:3, :]))
        v = tok[pl.ds(r * 24, 24)].astype(jnp.float32).reshape(48, 512) + ground + level
        emb[pl.ds(pl.multiple_of(r * 48, 16), 48), :] = v
        n = norm_groups([v[:, 128 * k:128 * k + 128] for k in range(4)], gain1[...])
        for k in range(4):
            e1[r, 4:52, 128 * k:128 * k + 128] = n[k]

    loop(12, row_norm)
    pack(hw1, e1, 12, own_rows, 4)
    pack(hn1, e1, 36, first_rows, 16)
    pack(hc1, e1, 12, first_rows, 4)
    halo1 = [neighbour(0, hw1, rw1, 0), neighbour(1, hn1, rn1, 1), neighbour(2, hc1, rc1, 2)]
    for c in halo1:
        c.start()

    n0.after_z()
    half = lambda axis: lax.broadcasted_iota(jnp.int32, (WT, 256), axis) >= WT // 2
    cut = (half(0) != half(1)) & (p.lat == 63)
    mask[0] = jnp.zeros((WT, 256), jnp.float32)
    mask[1] = jnp.where(cut, ABSENT, 0.0)
    b1.wait()
    prepare_bias(flat1, table1, 16)
    n0.after_y()
    n1.after_z()
    b2.wait()
    prepare_bias(flat2, table2, 32)

    n0.after_far()
    n2.after_z()
    n0.after_x()
    for c in halo1:
        c.wait_recv()

    unpack_rows(e1, rw1, 12, own_rows, 52)
    unpack_rows(e1, rn1, 36, next_rows, 16)
    unpack_rows(e1, rc1, 12, next_rows, 52)
    for w in range(4):
        a, b = w // 2, w % 2
        x1[WT * w:WT * w + WT, :] = e1[3 + 6 * a:9 + 6 * a, 16 + 24 * b:40 + 24 * b, :].reshape(
            WT, 512).astype(jnp.bfloat16)


    n1.after_y()
    n0.finish()
    def unpack(i):
        z, l = i // 4, 2 * (i % 4)
        both = [jnp.concatenate([full0[0, z, l + d], full0[1, z, l + d]], 1).astype(jnp.float32)
                for d in range(2)]
        qw[pl.ds(pl.multiple_of(48 * i, 16), 48), :] = jnp.concatenate(
            [both[0][:24], both[1][:24]], 0).astype(jnp.bfloat16)
        ow[pl.ds(pl.multiple_of(16 * i, 16), 16), :] = jnp.concatenate(
            [both[0][24:], both[1][24:]], 0).astype(jnp.bfloat16)

    loop(32, unpack)

    def project1(n):
        out = times(x1[...], qw[pl.ds(pl.multiple_of(256 * n, 256), 256), :]).astype(jnp.bfloat16)
        qkv1[2 * n] = out[:, :128]
        qkv1[2 * n + 1] = out[:, 128:]

    loop(6, project1)

    def attend1(i):
        w, g = 3 - i // 4, i % 4
        rows = pl.ds(pl.multiple_of(WT * w, 16), WT)
        heads = pl.ds(pl.multiple_of(4 * WT * g, 16), 4 * WT)
        out = attend(qkv1[g, rows, :], qkv1[4 + g, rows, :], qkv1[8 + g, rows, :],
                     table1[0, heads, :], table1[1, heads, :], mask[w // 2])
        e1[pl.ds(3 + 6 * (w // 2), 6), pl.ds(pl.multiple_of(16 + 24 * (w % 2), 8), 24),
           pl.ds(pl.multiple_of(128 * g, 128), 128)] = out.reshape(6, 24, 128)

    loop(8, attend1, 0, 2)
    pack(bn1, e1, 36, next_rows, 16)
    pack(bc1, e1, 12, next_rows, 52)
    back1 = [neighbour(3, bn1, sn1, 4), neighbour(4, bc1, sc1, 5)]
    for c in back1:
        c.start()
    loop(12, attend1, 8, 2)

    pack(bw1, e1, 12, own_rows, 52)
    back1.append(neighbour(5, bw1, sw1, 3))
    back1[2].start()
    n3.start()
    n1.after_far()
    n2.after_y()
    loop(16, attend1, 12, 2)
    n1.after_x()
    n3.after_z()
    for c in back1:
        c.wait_recv()

    unpack_rows(e1, sw1, 12, own_rows, 4)
    unpack_rows(e1, sn1, 36, first_rows, 16)
    unpack_rows(e1, sc1, 12, first_rows, 4)

    def collect1(r):
        x1[pl.ds(pl.multiple_of(48 * r, 16), 48), :] = e1[r, 4:52, :].astype(jnp.bfloat16)

    loop(12, collect1)
    for n in range(2):
        cols = slice(256 * n, 256 * n + 256)
        out = emb[:, cols] + times(x1[...], ow[cols, :])
        one[:, cols] = out.astype(jnp.bfloat16)
        s1[2 * n] = out[:, :128]
        s1[2 * n + 1] = out[:, 128:]

    def merge_rows(i):
        for dr in range(2):
            for dc in range(2):
                for level in range(2):
                    for k in range(4):
                        mg[(dc * 2 + dr) * 4 + k, pl.ds(24 * i + level, 12, stride=2), :] = s1[
                            k, pl.ds((2 * i + dr) * 48 + 2 * dc + level, 12, stride=4), :]

    loop(6, merge_rows)

    def merge_norm(c):
        rows = pl.ds(pl.multiple_of(48 * c, 16), 48)
        n = norm_groups([mg[k, rows, :] for k in range(16)], gain_merge[...])
        for k in range(16):
            mn[rows, 128 * k:128 * k + 128] = n[k].astype(jnp.bfloat16)

    loop(3, merge_norm)

    n1.finish()
    def merge_product(n):
        zs = pl.ds(2 * n, 2)
        out = times(mn[:, :1024], full1[0, zs].reshape(256, 1024))
        out = out + times(mn[:, 1024:], full1[1, zs].reshape(256, 1024))
        s2[2 * n] = out[:, :128]
        s2[2 * n + 1] = out[:, 128:]

    loop(4, merge_product)

    n2.after_far()
    def row_norm2(r):
        rows = pl.ds(pl.multiple_of(72 * r, 8), 72)
        n = norm_groups([s2[k, rows, :] for k in range(8)], gain2[...])
        for k in range(8):
            e2[pl.ds(3 * r, 3), 4:28, 128 * k:128 * k + 128] = n[k].reshape(3, 24, 128)

    loop(2, row_norm2)

    def pack2(out, r, first, lanes, width):
        for k in range(2):
            for i in range(3):
                at = 36 * k + 12 * i
                pad[at:at + 12, :width] = e2[r + i, first:first + 12, lanes + width * k:lanes + width * k + width]
        out[...] = pad[:80, :width].astype(jnp.bfloat16)

    def unpack2(came, r, first, lanes, width):
        pad[:80, :width] = came[...].astype(jnp.float32)
        for k in range(2):
            for i in range(3):
                at = 36 * k + 12 * i
                e2[r + i, first:first + 12, lanes + width * k:lanes + width * k + width] = pad[at:at + 12, :width]

    pack2(hw2, 3, 4, 0, 512)
    pack2(hn2, 0, 16, 0, 512)
    pack2(hc2, 0, 4, 0, 512)
    halo2 = [neighbour(6, hw2, rw2, 0), neighbour(7, hn2, rn2, 1), neighbour(8, hc2, rc2, 2)]
    for c in halo2:
        c.start()
    n2.after_x()
    n3.after_y()
    for c in halo2:
        c.wait_recv()
    unpack2(rw2, 3, 28, 0, 512)
    unpack2(rn2, 6, 16, 0, 512)
    unpack2(rc2, 6, 28, 0, 512)
    x2[...] = e2[3:9, 16:40, :].reshape(WT, 1024).astype(jnp.bfloat16)


    n2.finish()
    def project2(z):
        first, second = [full2[h, z].reshape(384, 512) for h in range(2)]
        out = (times(x2[:, :512], first) + times(x2[:, 512:], second)).astype(jnp.bfloat16)
        for k in range(3):
            qkv2[3 * z + k] = out[:, 128 * k:128 * k + 128]

    loop(8, project2)

    def attend2(g):
        heads = pl.ds(pl.multiple_of(4 * WT * g, 16), 4 * WT)
        out = attend(qkv2[g], qkv2[8 + g], qkv2[16 + g], table2[0, heads, :], table2[1, heads, :], mask[1])
        e2[3:9, 16:40, pl.ds(pl.multiple_of(128 * g, 128), 128)] = out.reshape(6, 24, 128)

    back2 = []
    for h in range(2):
        loop(4 * h + 4, attend2, 4 * h, 2)
        pack2(bw2.at[h], 3, 28, 512 * h, 256)
        pack2(bn2.at[h], 6, 16, 512 * h, 256)
        pack2(bc2.at[h], 6, 28, 512 * h, 256)
        some = [neighbour(9 + 3 * h, bw2.at[h], sw2.at[h], 3), neighbour(10 + 3 * h, bn2.at[h], sn2.at[h], 4),
                neighbour(11 + 3 * h, bc2.at[h], sc2.at[h], 5)]
        for c in some:
            c.start()
        if h == 0:
            n3.after_far()
        back2 += some
    n3.after_x()
    n3.finish()
    for c in back2:
        c.wait_recv()
    for h in range(2):
        unpack2(sw2.at[h], 3, 4, 512 * h, 256)
        unpack2(sn2.at[h], 0, 16, 512 * h, 256)
        unpack2(sc2.at[h], 0, 4, 512 * h, 256)
    for r in range(6):
        x2[24 * r:24 * r + 24, :] = e2[r, 4:28, :].astype(jnp.bfloat16)

    def last(n):
        zs = pl.ds(2 * n, 2)
        out = times(x2[:, :512], full3[0, zs].reshape(256, 512))
        out = out + times(x2[:, 512:], full3[1, zs].reshape(256, 512))
        out = out + jnp.concatenate([s2[2 * n], s2[2 * n + 1]], 1)
        two[:, pl.ds(pl.multiple_of(256 * n, 256), 256)] = out.astype(jnp.bfloat16)

    loop(4, last)
    for c in halo1 + back1 + halo2 + back2:
        c.wait_send()
    for net in nets:
        net.drain()


def shards(
    tokens, land_sea, surface_embed, level_table, level_embed, gain1, w_qkv1, bias1, w_out1,
    gain_merge, w_merge, gain2, w_qkv2, bias2, w_out2,
):
    f32, bf16 = jnp.float32, jnp.bfloat16
    shapes = [(2, 8, 8, rows, depth // 2) for rows, depth in GROUPS]
    level1 = [((112, 512), bf16), ((112, 512), bf16), ((48, 512), bf16)]
    operands = (
        tokens.reshape(288, 2, 512), land_sea, surface_embed, level_table, level_embed, gain1[None], w_qkv1.T,
        w_out1.T, gain_merge[None], w_merge.T, gain2[None], w_qkv2.T, w_out2.T, bias1, bias2)
    scratch = [pltpu.VMEM(a.shape, a.dtype) for i, a in enumerate(operands[:13]) if i != 3]
    scratch += [pltpu.VMEM((576, 512), f32)] + [pltpu.VMEM(s, bf16) for s in shapes] + [pltpu.VMEM(s, t) for s, t in (
        ((16, WT * WT), f32), ((32, WT * WT), f32),
        ((2, 16 * WT, 128), f32), ((2, 32 * WT, 128), f32), ((2, WT, 256), f32),
        ((112, 512), f32), ((15, 64, 512), f32), *level1, *level1, *level1,
        ((1536, 512), bf16), ((512, 512), bf16), ((576, 512), bf16), ((12, 576, 128), bf16),
        ((4, 576, 128), f32), ((16, WT, 128), f32), ((WT, 2048), bf16),
        ((8, WT, 128), f32), ((9, 40, 1024), f32), *[((80, 512), bf16)] * 6, *[((2, 80, 256), bf16)] * 3,
        ((WT, 1024), bf16), ((24, WT, 128), bf16),
        *level1, *[((2, 80, 256), bf16)] * 3,
    )] + [
        pltpu.SemaphoreType.DMA((NG, SLOTS)), pltpu.SemaphoreType.DMA((NG, SLOTS)),
        pltpu.SemaphoreType.DMA((15,)), pltpu.SemaphoreType.DMA((15,)), pltpu.SemaphoreType.DMA((14,)),
    ]
    vmem, anywhere = pl.BlockSpec(memory_space=pltpu.VMEM), pl.BlockSpec(memory_space=pl.ANY)
    one, two = pl.pallas_call(
        block_kernel,
        out_shape=[jax.ShapeDtypeStruct((576, 512), bf16), jax.ShapeDtypeStruct((WT, 1024), bf16)],
        in_specs=[anywhere] * 3 + [pl.BlockSpec(memory_space=pltpu.SMEM)] + [anywhere] * 11,
        out_specs=[vmem] * 2,
        scratch_shapes=scratch,
        compiler_params=pltpu.CompilerParams(
            collective_id=0, has_side_effects=True, vmem_limit_bytes=60 * 2**20),
    )(*operands)
    return one.reshape(12, 24, 2, 512), two.reshape(6, 12, 2, 1024)


def solution(mesh):
    placed = (
        P("lat", "lon", None, None), P("lat", "lon"), P(), P(), P(), P(),
        P(None, "lat"), P(), P(None, "lat"), P(), P(None, "lat"), P(), P(None, "lat"), P(), P(None, "lat"),
    )
    return jax.shard_map(
        shards,
        mesh=mesh,
        in_specs=placed,
        out_specs=(P("lat", "lon", None, None), P("lat", "lon", None, None)),
        check_vma=False,
    )
```

```python
import jax
import jax.numpy as jnp
from jax import lax
from jax.experimental import pallas as pl
from jax.experimental.pallas import tpu as pltpu
from jax.sharding import PartitionSpec as P

WT = 144
NT = (((1,), (1,)), ((), ()))
LOG2E = 1.4426950408889634
ABSENT = -1e30
MESH = pl.DeviceIdType.MESH
GROUPS = ((32, 512), (16, 2048), (48, 1024), (16, 1024))
NG = len(GROUPS)
ZS, YS, XS, SS = 0, 7, 15, 23
SLOTS = 36


class Place:
    def __init__(self):
        lat = lax.axis_index("lat")
        lon = lax.axis_index("lon")
        self.lat, self.lon = lat, lon
        self.z = lat // 8
        self.xlo = (lat // 4) % 2
        self.y = lat % 4
        self.xhi = lon // 2
        self.core = lon % 2
        self.x = self.xhi * 2 + self.xlo

    def at(self, x=None, y=None, z=None, core=None):
        x = self.x if x is None else x
        y = self.y if y is None else y
        z = self.z if z is None else z
        core = self.core if core is None else core
        return ((z * 2 + x % 2) * 4 + y, (x // 2) * 2 + core)


class Gather:
    def __init__(self, place, g, full, send, recv):
        p = place
        self.p, self.g, self.full, self.send, self.recv = p, g, full, send, recv
        self.up = p.at(y=(p.y + 1) % 4)
        self.down = p.at(y=(p.y + 3) % 4)
        self.east = p.at(x=(p.x + 1) % 4)
        self.west = p.at(x=(p.x + 3) % 4)
        self.twin = p.at(core=1 - p.core)
        self.partners = [p.at(z=(p.z + d) % 8) for d in range(1, 8)] + [
            self.up, self.down, self.east, self.west, self.twin, p.at(y=(p.y + 2) % 4)]
        self.sent = []

    def copy(self, slot, part, to):
        return pltpu.make_async_remote_copy(
            src_ref=part, dst_ref=part, send_sem=self.send.at[self.g, slot],
            recv_sem=self.recv.at[self.g, slot], device_id=to, device_id_type=MESH)

    def part(self, half, zs, line):
        return self.full.at[half, zs, line]

    def move(self, slot, to, zs, line):
        c = self.copy(slot, self.part(self.p.core, zs, line), to)
        c.start()
        self.sent.append(c)

    def landed(self, slot, zs, line, half=None):
        self.copy(slot, self.part(self.p.core if half is None else half, zs, line), self.twin).wait_recv()

    def line(self, other, dy):
        xlo = 1 - self.p.xlo if other else self.p.xlo
        return xlo * 4 + (self.p.y + dy) % 4

    def drain(self):
        for c in self.sent:
            c.wait_send()

    whole = pl.ds(0, 8)
    parts = (pl.ds(0, 4), pl.ds(4, 4))

    def start(self):
        p = self.p
        for d in range(1, 8):
            self.move(ZS + d - 1, p.at(z=(p.z + d) % 8), p.z, self.line(0, 0))

    def z_landed(self):
        p = self.p
        for d in range(1, 8):
            self.landed(ZS + d - 1, (p.z + 8 - d) % 8, self.line(0, 0))

    def after_z(self):
        self.z_landed()
        own = self.line(0, 0)
        self.move(YS + 0, self.up, self.whole, own)
        self.move(YS + 1, self.down, self.whole, own)
        self.to_x(0, 0)
        self.to_x(0, 1)
        self.move(SS + 0, self.twin, self.whole, own)

    def to_x(self, dy, part):
        self.move(XS + 2 * dy + part, (self.east, self.west)[part], self.parts[part], self.line(0, dy))

    def after_y(self):
        below, above = self.line(0, 3), self.line(0, 1)
        self.landed(YS + 0, self.whole, below)
        self.move(YS + 2, self.up, self.parts[0], below)
        self.landed(YS + 1, self.whole, above)
        self.move(YS + 3, self.down, self.parts[1], above)
        for dy in (3, 1):
            for part in (0, 1):
                self.to_x(dy, part)
        self.move(SS + 1, self.twin, self.whole, below)
        self.move(SS + 2, self.twin, self.whole, above)

    def after_far(self):
        for part in (0, 1):
            self.landed(YS + 2 + part, self.parts[part], self.line(0, 2))
            self.to_x(2, part)
            self.move(SS + 3 + part, self.twin, self.parts[part], self.line(0, 2))

    def after_x(self):
        for dy in (0, 3, 1, 2):
            for part in (0, 1):
                self.landed(XS + 2 * dy + part, self.parts[part], self.line(1, dy))
                self.move(SS + 5 + 2 * dy + part, self.twin, self.parts[part], self.line(1, dy))

    def finish(self):
        half = 1 - self.p.core
        self.landed(SS + 0, self.whole, self.line(0, 0), half)
        self.landed(SS + 1, self.whole, self.line(0, 3), half)
        self.landed(SS + 2, self.whole, self.line(0, 1), half)
        for part in (0, 1):
            self.landed(SS + 3 + part, self.parts[part], self.line(0, 2), half)
            for dy in range(4):
                self.landed(SS + 5 + 2 * dy + part, self.parts[part], self.line(1, dy), half)


class GatherZXY(Gather):
    def after_z(self):
        self.z_landed()
        own = self.line(0, 0)
        self.to_x(0, 0)
        self.to_x(0, 1)
        self.move(YS + 0, self.up, self.whole, own)
        self.move(YS + 1, self.down, self.whole, own)
        self.move(SS + 0, self.twin, self.whole, own)

    def after_x(self):
        other = self.line(1, 0)
        for part in (0, 1):
            self.landed(XS + part, self.parts[part], other)
        self.move(YS + 4, self.up, self.whole, other)
        self.move(YS + 5, self.down, self.whole, other)
        self.move(SS + 5, self.twin, self.whole, other)

    def after_y(self):
        for k in (0, 1):
            below, above = self.line(k, 3), self.line(k, 1)
            self.landed(YS + 4 * k, self.whole, below)
            self.move(YS + 4 * k + 2, self.up, self.parts[0], below)
            self.landed(YS + 4 * k + 1, self.whole, above)
            self.move(YS + 4 * k + 3, self.down, self.parts[1], above)
            self.move(SS + 5 * k + 1, self.twin, self.whole, below)
            self.move(SS + 5 * k + 2, self.twin, self.whole, above)

    def after_far(self):
        for k in (0, 1):
            for part in (0, 1):
                self.landed(YS + 4 * k + 2 + part, self.parts[part], self.line(k, 2))
                self.move(SS + 5 * k + 3 + part, self.twin, self.parts[part], self.line(k, 2))

    def finish(self):
        half = 1 - self.p.core
        for k in (0, 1):
            self.landed(SS + 5 * k, self.whole, self.line(k, 0), half)
            self.landed(SS + 5 * k + 1, self.whole, self.line(k, 3), half)
            self.landed(SS + 5 * k + 2, self.whole, self.line(k, 1), half)
            for part in (0, 1):
                self.landed(SS + 5 * k + 3 + part, self.parts[part], self.line(k, 2), half)


class GatherXYZ(Gather):
    def quarter(self, part):
        depth = self.full.shape[-1] // 2
        return pl.ds(0, self.full.shape[-2]), pl.ds(part * depth, depth)

    def start(self):
        p = self.p
        for part in (0, 1):
            mine = self.full.at[p.core, p.z, self.line(0, 0)].at[self.quarter(part)]
            c = self.copy(XS + part, mine, (self.east, self.west)[part])
            c.start()
            self.sent.append(c)

    def after_x(self):
        p = self.p
        for part in (0, 1):
            other = self.full.at[p.core, p.z, self.line(1, 0)].at[self.quarter(part)]
            self.copy(XS + part, other, self.twin).wait_recv()
        for k in (0, 1):
            for d in range(1, 4):
                self.move(YS + 3 * k + d - 1, p.at(y=(p.y + d) % 4), p.z, self.line(k, 0))

    def after_y(self):
        p = self.p
        for k in (0, 1):
            for d in range(1, 4):
                self.landed(YS + 3 * k + d - 1, p.z, self.line(k, 4 - d))
        for d in range(1, 8):
            self.move(ZS + d - 1, p.at(z=(p.z + d) % 8), p.z, self.whole)
        self.move(SS + 0, self.twin, p.z, self.whole)

    def after_z(self):
        p = self.p
        for d in range(1, 8):
            self.landed(ZS + d - 1, (p.z + 8 - d) % 8, self.whole)
            self.move(SS + d, self.twin, (p.z + 8 - d) % 8, self.whole)

    def finish(self):
        p = self.p
        for d in range(8):
            self.landed(SS + d, (p.z + 8 - d) % 8, self.whole, 1 - p.core)


def times(a, b):
    return lax.dot_general(a, b, NT, preferred_element_type=jnp.float32)


def norm_groups(parts, gain):
    width = 128 * len(parts)
    mean = jnp.sum(sum(parts), -1, keepdims=True) / width
    parts = [p - mean for p in parts]
    spread = jnp.sum(sum(p * p for p in parts), -1, keepdims=True) / width
    scale = lax.rsqrt(spread + 1e-05)
    return [p * scale * gain[:, 128 * k:128 * k + 128] for k, p in enumerate(parts)]


def prepare_bias(flat, table, heads):
    lane = lax.broadcasted_iota(jnp.int32, (8, 128), 1)

    def eight(i, _):
        t, q = i // 18, i % 18
        rows = pl.ds(pl.multiple_of(t * 8, 8), 8)
        block = flat[rows, pl.ds(pl.multiple_of(q * 1152, 128), 1152)] * LOG2E
        for s in range(8):
            first, second = block[:, 128 * s:128 * s + 128], block[:, 128 * s + 128:128 * s + 256]
            if s:
                first, second = pltpu.roll(first, 128 - 16 * s, 1), pltpu.roll(second, 128 - 16 * s, 1)
                first = jnp.where(lane < 128 - 16 * s, first, second)
            second = jnp.where(lane < 16, second, ABSENT)
            where = pl.ds(t * 8 * WT + q * 8 + s, 8, stride=WT)
            table[0, where, :] = first
            table[1, where, :] = second
        return 0

    lax.fori_loop(0, heads // 8 * 18, eight, 0)


def attend(q, k, v, bias0, bias1, mask):
    lane = lax.broadcasted_iota(jnp.int32, (WT, 128), 1) // 32
    none = jnp.zeros((256 - WT, 128), jnp.bfloat16)
    heads = jnp.concatenate([jnp.where(lane == h, q, jnp.zeros_like(q)) for h in range(4)], 0)
    scores = times(heads, jnp.concatenate([k, none], 0)) * (LOG2E / 32 ** 0.5)
    bias = jnp.concatenate([bias0, bias1], 1)
    scores = scores + bias + jnp.concatenate([mask] * 4, 0)
    top = jnp.max(scores, -1, keepdims=True)
    weights = jnp.exp2(scores - top).astype(jnp.bfloat16)
    values = jnp.concatenate([jnp.concatenate([v, none], 0), jnp.ones((256, 128), jnp.bfloat16)], 1)
    mixed = jnp.dot(weights, values, preferred_element_type=jnp.float32)
    total, over = mixed[:WT, :128], mixed[:WT, 128:]
    for h in range(1, 4):
        total = jnp.where(lane == h, mixed[WT * h:WT * h + WT, :128], total)
        over = jnp.where(lane == h, mixed[WT * h:WT * h + WT, 128:], over)
    return total / over


def loop(count, step, first=0, unroll=1):
    lax.fori_loop(first, count, lambda i, c: (step(i), c)[1], 0, unroll=unroll)


def block_kernel(
    tok_hbm, land_hbm, surface_hbm, table, levels_hbm, gain1_hbm, wqkv1_hbm, wout1_hbm, gain_merge_hbm,
    wmerge_hbm, gain2_hbm, wqkv2_hbm, wout2_hbm, bias1_hbm, bias2_hbm,
    one, two,
    tok, land, surface, levels, gain1, wqkv1, wout1, gain_merge, wmerge, gain2, wqkv2, wout2,
    emb,
    full0, full1, full2, full3, flat1, flat2, table1, table2, mask,
    pad, e1, hw1, hn1, hc1, rw1, rn1, rc1, bw1, bn1, bc1, qw, ow, x1, qkv1, s1, mg, mn,
    s2, e2, hw2, hn2, hc2, rw2, rn2, rc2, bw2, bn2, bc2, x2, qkv2,
    sw1, sn1, sc1, sw2, sn2, sc2,
    send, recv, hsend, hrecv, local,
):
    p = Place()
    full = (full0, full1, full2, full3)
    kinds = (Gather, Gather, Gather, Gather)
    n0, n1, n2, n3 = nets = [kinds[g](p, g, full[g], send, recv) for g in range(NG)]
    north, south = (p.lat + 63) % 64, (p.lat + 1) % 64
    west, east = (p.lon + 3) % 4, (p.lon + 1) % 4
    around = [(p.lat, west), (north, p.lon), (north, west), (p.lat, east), (south, p.lon), (south, east)]
    partners = n0.partners + around
    barrier = pltpu.get_barrier_semaphore()
    for to in partners:
        pl.semaphore_signal(barrier, inc=1, device_id=to, device_id_type=MESH)
    pairs = (
        (wqkv1_hbm, wqkv1), (wout1_hbm, wout1), (tok_hbm, tok), (land_hbm, land), (surface_hbm, surface),
        (levels_hbm, levels), (gain1_hbm, gain1), (wmerge_hbm, wmerge), (wqkv2_hbm, wqkv2), (wout2_hbm, wout2),
        (gain_merge_hbm, gain_merge), (gain2_hbm, gain2))
    inputs = [pltpu.make_async_copy(src, dst, local.at[2 + i]) for i, (src, dst) in enumerate(pairs)]
    for c in inputs:
        c.start()
    b1 = pltpu.make_async_copy(bias1_hbm, flat1, local.at[0])
    b2 = pltpu.make_async_copy(bias2_hbm, flat2, local.at[1])
    b1.start()
    b2.start()

    for c in inputs:
        c.wait()

    own = n0.line(0, 0)

    def halved(w):
        depth = w.shape[1] // 2
        return w[:, pl.ds(pl.multiple_of(p.core * depth, depth), depth)]

    full0[p.core, p.z, own] = jnp.concatenate(
        [halved(wqkv1).astype(jnp.float32), halved(wout1).astype(jnp.float32)], 0).astype(jnp.bfloat16)
    full1[p.core, p.z, own] = halved(wmerge)
    full2[p.core, p.z, own] = halved(wqkv2)
    full3[p.core, p.z, own] = halved(wout2)
    pl.semaphore_wait(barrier, len(partners))

    def neighbour(slot, src, dst, way):
        return pltpu.make_async_remote_copy(
            src_ref=src, dst_ref=dst, send_sem=hsend.at[slot], recv_sem=hrecv.at[slot],
            device_id=around[way], device_id_type=MESH)


    n0.start()
    n1.start()
    n2.start()

    def pack(out, source, count, rows, first):
        for i, r in enumerate(rows):
            pad[count * i:count * i + count, :] = source[r, first:first + count, :]
        out[...] = pad[:out.shape[0], :].astype(jnp.bfloat16)

    def unpack_rows(target, came, count, rows, first):
        pad[:came.shape[0], :] = came[...].astype(jnp.float32)
        for i, r in enumerate(rows):
            target[r, first:first + count, :] = pad[count * i:count * i + count, :]

    pad[...] = jnp.zeros((112, 512), jnp.float32)
    own_rows, first_rows, next_rows = range(3, 12), range(3), range(12, 15)

    numbers = lax.broadcasted_iota(jnp.int32, levels.shape, 0)
    rows = [jnp.sum(jnp.where(numbers == table[i], levels[...], 0.0), 0, keepdims=True) for i in range(2)]
    level = jnp.where(lax.broadcasted_iota(jnp.int32, (48, 512), 0) % 2 == 0, rows[0], rows[1])
    patch = lax.broadcasted_iota(jnp.int32, (48, 24), 0) // 2 == lax.broadcasted_iota(jnp.int32, (48, 24), 1)

    def row_norm(r):
        kinds = land[pl.ds(r, 1), :].astype(jnp.float32)
        kind = jnp.sum(jnp.where(patch, kinds, 0.0), -1, keepdims=True)
        ground = jnp.where(kind == 0.0, surface[0:1, :], jnp.where(kind == 1.0, surface[1:2, :], surface[2:3, :]))
        v = tok[pl.ds(r * 24, 24)].astype(jnp.float32).reshape(48, 512) + ground + level
        emb[pl.ds(pl.multiple_of(r * 48, 16), 48), :] = v
        n = norm_groups([v[:, 128 * k:128 * k + 128] for k in range(4)], gain1[...])
        for k in range(4):
            e1[r, 4:52, 128 * k:128 * k + 128] = n[k]

    loop(12, row_norm)
    pack(hw1, e1, 12, own_rows, 4)
    pack(hn1, e1, 36, first_rows, 16)
    pack(hc1, e1, 12, first_rows, 4)
    halo1 = [neighbour(0, hw1, rw1, 0), neighbour(1, hn1, rn1, 1), neighbour(2, hc1, rc1, 2)]
    for c in halo1:
        c.start()

    n0.after_z()
    half = lambda axis: lax.broadcasted_iota(jnp.int32, (WT, 256), axis) >= WT // 2
    cut = (half(0) != half(1)) & (p.lat == 63)
    mask[0] = jnp.zeros((WT, 256), jnp.float32)
    mask[1] = jnp.where(cut, ABSENT, 0.0)
    b1.wait()
    prepare_bias(flat1, table1, 16)
    n0.after_y()
    n1.after_z()
    b2.wait()
    prepare_bias(flat2, table2, 32)

    n0.after_far()
    n2.after_z()
    n0.after_x()
    for c in halo1:
        c.wait_recv()

    unpack_rows(e1, rw1, 12, own_rows, 52)
    unpack_rows(e1, rn1, 36, next_rows, 16)
    unpack_rows(e1, rc1, 12, next_rows, 52)
    for w in range(4):
        a, b = w // 2, w % 2
        x1[WT * w:WT * w + WT, :] = e1[3 + 6 * a:9 + 6 * a, 16 + 24 * b:40 + 24 * b, :].reshape(
            WT, 512).astype(jnp.bfloat16)


    n1.after_y()
    n0.finish()
    def unpack(i):
        z, l = i // 4, 2 * (i % 4)
        both = [jnp.concatenate([full0[0, z, l + d], full0[1, z, l + d]], 1).astype(jnp.float32)
                for d in range(2)]
        qw[pl.ds(pl.multiple_of(48 * i, 16), 48), :] = jnp.concatenate(
            [both[0][:24], both[1][:24]], 0).astype(jnp.bfloat16)
        ow[pl.ds(pl.multiple_of(16 * i, 16), 16), :] = jnp.concatenate(
            [both[0][24:], both[1][24:]], 0).astype(jnp.bfloat16)

    loop(32, unpack)

    def project1(n):
        out = times(x1[...], qw[pl.ds(pl.multiple_of(256 * n, 256), 256), :]).astype(jnp.bfloat16)
        qkv1[2 * n] = out[:, :128]
        qkv1[2 * n + 1] = out[:, 128:]

    loop(6, project1)

    def attend1(i):
        w, g = 3 - i // 4, i % 4
        rows = pl.ds(pl.multiple_of(WT * w, 16), WT)
        heads = pl.ds(pl.multiple_of(4 * WT * g, 16), 4 * WT)
        out = attend(qkv1[g, rows, :], qkv1[4 + g, rows, :], qkv1[8 + g, rows, :],
                     table1[0, heads, :], table1[1, heads, :], mask[w // 2])
        e1[pl.ds(3 + 6 * (w // 2), 6), pl.ds(pl.multiple_of(16 + 24 * (w % 2), 8), 24),
           pl.ds(pl.multiple_of(128 * g, 128), 128)] = out.reshape(6, 24, 128)

    loop(8, attend1, 0, 2)
    pack(bn1, e1, 36, next_rows, 16)
    pack(bc1, e1, 12, next_rows, 52)
    back1 = [neighbour(3, bn1, sn1, 4), neighbour(4, bc1, sc1, 5)]
    for c in back1:
        c.start()
    loop(12, attend1, 8, 2)

    pack(bw1, e1, 12, own_rows, 52)
    back1.append(neighbour(5, bw1, sw1, 3))
    back1[2].start()
    n3.start()
    n1.after_far()
    n2.after_y()
    loop(16, attend1, 12, 2)
    n1.after_x()
    n3.after_z()
    for c in back1:
        c.wait_recv()

    unpack_rows(e1, sw1, 12, own_rows, 4)
    unpack_rows(e1, sn1, 36, first_rows, 16)
    unpack_rows(e1, sc1, 12, first_rows, 4)

    def collect1(r):
        x1[pl.ds(pl.multiple_of(48 * r, 16), 48), :] = e1[r, 4:52, :].astype(jnp.bfloat16)

    loop(12, collect1)
    for n in range(2):
        cols = slice(256 * n, 256 * n + 256)
        out = emb[:, cols] + times(x1[...], ow[cols, :])
        one[:, cols] = out.astype(jnp.bfloat16)
        s1[2 * n] = out[:, :128]
        s1[2 * n + 1] = out[:, 128:]

    def merge_rows(i):
        for dr in range(2):
            for dc in range(2):
                for level in range(2):
                    for k in range(4):
                        mg[(dc * 2 + dr) * 4 + k, pl.ds(24 * i + level, 12, stride=2), :] = s1[
                            k, pl.ds((2 * i + dr) * 48 + 2 * dc + level, 12, stride=4), :]

    loop(6, merge_rows)

    def merge_norm(c):
        rows = pl.ds(pl.multiple_of(48 * c, 16), 48)
        n = norm_groups([mg[k, rows, :] for k in range(16)], gain_merge[...])
        for k in range(16):
            mn[rows, 128 * k:128 * k + 128] = n[k].astype(jnp.bfloat16)

    loop(3, merge_norm)

    n1.finish()
    def merge_product(n):
        zs = pl.ds(2 * n, 2)
        out = times(mn[:, :1024], full1[0, zs].reshape(256, 1024))
        out = out + times(mn[:, 1024:], full1[1, zs].reshape(256, 1024))
        s2[2 * n] = out[:, :128]
        s2[2 * n + 1] = out[:, 128:]

    loop(4, merge_product)

    n2.after_far()
    def row_norm2(r):
        rows = pl.ds(pl.multiple_of(72 * r, 8), 72)
        n = norm_groups([s2[k, rows, :] for k in range(8)], gain2[...])
        for k in range(8):
            e2[pl.ds(3 * r, 3), 4:28, 128 * k:128 * k + 128] = n[k].reshape(3, 24, 128)

    loop(2, row_norm2)

    def pack2(out, r, first, lanes, width):
        for k in range(2):
            for i in range(3):
                at = 36 * k + 12 * i
                pad[at:at + 12, :width] = e2[r + i, first:first + 12, lanes + width * k:lanes + width * k + width]
        out[...] = pad[:80, :width].astype(jnp.bfloat16)

    def unpack2(came, r, first, lanes, width):
        pad[:80, :width] = came[...].astype(jnp.float32)
        for k in range(2):
            for i in range(3):
                at = 36 * k + 12 * i
                e2[r + i, first:first + 12, lanes + width * k:lanes + width * k + width] = pad[at:at + 12, :width]

    pack2(hw2, 3, 4, 0, 512)
    pack2(hn2, 0, 16, 0, 512)
    pack2(hc2, 0, 4, 0, 512)
    halo2 = [neighbour(6, hw2, rw2, 0), neighbour(7, hn2, rn2, 1), neighbour(8, hc2, rc2, 2)]
    for c in halo2:
        c.start()
    n2.after_x()
    n3.after_y()
    for c in halo2:
        c.wait_recv()
    unpack2(rw2, 3, 28, 0, 512)
    unpack2(rn2, 6, 16, 0, 512)
    unpack2(rc2, 6, 28, 0, 512)
    x2[...] = e2[3:9, 16:40, :].reshape(WT, 1024).astype(jnp.bfloat16)


    n2.finish()
    def project2(z):
        first, second = [full2[h, z].reshape(384, 512) for h in range(2)]
        out = (times(x2[:, :512], first) + times(x2[:, 512:], second)).astype(jnp.bfloat16)
        for k in range(3):
            qkv2[3 * z + k] = out[:, 128 * k:128 * k + 128]

    loop(8, project2)

    def attend2(g):
        heads = pl.ds(pl.multiple_of(4 * WT * g, 16), 4 * WT)
        out = attend(qkv2[g], qkv2[8 + g], qkv2[16 + g], table2[0, heads, :], table2[1, heads, :], mask[1])
        e2[3:9, 16:40, pl.ds(pl.multiple_of(128 * g, 128), 128)] = out.reshape(6, 24, 128)

    back2 = []
    for h in range(2):
        loop(4 * h + 4, attend2, 4 * h, 2)
        pack2(bw2.at[h], 3, 28, 512 * h, 256)
        pack2(bn2.at[h], 6, 16, 512 * h, 256)
        pack2(bc2.at[h], 6, 28, 512 * h, 256)
        some = [neighbour(9 + 3 * h, bw2.at[h], sw2.at[h], 3), neighbour(10 + 3 * h, bn2.at[h], sn2.at[h], 4),
                neighbour(11 + 3 * h, bc2.at[h], sc2.at[h], 5)]
        for c in some:
            c.start()
        if h == 0:
            n3.after_far()
        back2 += some
    n3.after_x()
    n3.finish()
    for h in range(2):
        for c in back2[3 * h:3 * h + 3]:
            c.wait_recv()
        unpack2(sw2.at[h], 3, 4, 512 * h, 256)
        unpack2(sn2.at[h], 0, 16, 512 * h, 256)
        unpack2(sc2.at[h], 0, 4, 512 * h, 256)
        cols = slice(512 * h, 512 * h + 512)
        for r in range(6):
            x2[24 * r:24 * r + 24, cols] = e2[r, 4:28, cols].astype(jnp.bfloat16)

        def last(n):
            out = times(x2[:, cols], full3[h, pl.ds(2 * n, 2)].reshape(256, 512))
            out = out + jnp.concatenate([s2[2 * n], s2[2 * n + 1]], 1)
            if h == 0:
                s2[2 * n] = out[:, :128]
                s2[2 * n + 1] = out[:, 128:]
            else:
                two[:, pl.ds(pl.multiple_of(256 * n, 256), 256)] = out.astype(jnp.bfloat16)

        loop(4, last)
    for c in halo1 + back1 + halo2 + back2:
        c.wait_send()
    for net in nets:
        net.drain()


def shards(
    tokens, land_sea, surface_embed, level_table, level_embed, gain1, w_qkv1, bias1, w_out1,
    gain_merge, w_merge, gain2, w_qkv2, bias2, w_out2,
):
    f32, bf16 = jnp.float32, jnp.bfloat16
    shapes = [(2, 8, 8, rows, depth // 2) for rows, depth in GROUPS]
    level1 = [((112, 512), bf16), ((112, 512), bf16), ((48, 512), bf16)]
    operands = (
        tokens.reshape(288, 2, 512), land_sea, surface_embed, level_table, level_embed, gain1[None], w_qkv1.T,
        w_out1.T, gain_merge[None], w_merge.T, gain2[None], w_qkv2.T, w_out2.T, bias1, bias2)
    scratch = [pltpu.VMEM(a.shape, a.dtype) for i, a in enumerate(operands[:13]) if i != 3]
    scratch += [pltpu.VMEM((576, 512), f32)] + [pltpu.VMEM(s, bf16) for s in shapes] + [pltpu.VMEM(s, t) for s, t in (
        ((16, WT * WT), f32), ((32, WT * WT), f32),
        ((2, 16 * WT, 128), f32), ((2, 32 * WT, 128), f32), ((2, WT, 256), f32),
        ((112, 512), f32), ((15, 64, 512), f32), *level1, *level1, *level1,
        ((1536, 512), bf16), ((512, 512), bf16), ((576, 512), bf16), ((12, 576, 128), bf16),
        ((4, 576, 128), f32), ((16, WT, 128), f32), ((WT, 2048), bf16),
        ((8, WT, 128), f32), ((9, 40, 1024), f32), *[((80, 512), bf16)] * 6, *[((2, 80, 256), bf16)] * 3,
        ((WT, 1024), bf16), ((24, WT, 128), bf16),
        *level1, *[((2, 80, 256), bf16)] * 3,
    )] + [
        pltpu.SemaphoreType.DMA((NG, SLOTS)), pltpu.SemaphoreType.DMA((NG, SLOTS)),
        pltpu.SemaphoreType.DMA((15,)), pltpu.SemaphoreType.DMA((15,)), pltpu.SemaphoreType.DMA((14,)),
    ]
    vmem, anywhere = pl.BlockSpec(memory_space=pltpu.VMEM), pl.BlockSpec(memory_space=pl.ANY)
    one, two = pl.pallas_call(
        block_kernel,
        out_shape=[jax.ShapeDtypeStruct((576, 512), bf16), jax.ShapeDtypeStruct((WT, 1024), bf16)],
        in_specs=[anywhere] * 3 + [pl.BlockSpec(memory_space=pltpu.SMEM)] + [anywhere] * 11,
        out_specs=[vmem] * 2,
        scratch_shapes=scratch,
        compiler_params=pltpu.CompilerParams(
            collective_id=0, has_side_effects=True, vmem_limit_bytes=60 * 2**20),
    )(*operands)
    return one.reshape(12, 24, 2, 512), two.reshape(6, 12, 2, 1024)


def solution(mesh):
    placed = (
        P("lat", "lon", None, None), P("lat", "lon"), P(), P(), P(), P(),
        P(None, "lat"), P(), P(None, "lat"), P(), P(None, "lat"), P(), P(None, "lat"), P(), P(None, "lat"),
    )
    return jax.shard_map(
        shards,
        mesh=mesh,
        in_specs=placed,
        out_specs=(P("lat", "lon", None, None), P("lat", "lon", None, None)),
        check_vma=False,
    )
```
